512 devices in a mesh: dp: 16 (over y, core), ctx: 32 (over x, z).
Axes of the slice: x: 4, y: 8, z: 8, core: 2. Of those that a mesh axis runs over, the one named last changes fastest.
Arguments:
- inputs: bfloat16 [16, 6144, 1536], P('dp', 'ctx'), may hold values from -6 to 6
- cotangent: bfloat16 [16, 6144, 1536], P('dp', 'ctx'), may hold values from -6 to 6
- conv_kernel: float32 [31, 1536], replicated, may hold values from -1 to 1
- norm_gain: float32 [1536], replicated, may hold values from 0.5 to 1.5
- adapt_down: bfloat16 [64, 1536, 128], P('ctx'), may hold values from -0.15625 to 0.15625
- adapt_up: bfloat16 [64, 128, 1536], P('ctx'), may hold values from -0.5 to 0.5
- segment_lengths: int32 [16, 32, 16], P('dp', 'ctx'), may hold values from 1 to 15, 192 in all within a row
- segment_langs: int32 [16, 32, 16], P('dp', 'ctx'), may hold values from 0 to 63, as said below
- lang_slot: int32 [64], replicated, may hold values from 0 to 63, as said below
Outputs:
- output: bfloat16 [16, 6144, 1536], P('dp', 'ctx')
- grad_input: bfloat16 [16, 6144, 1536], P('dp', 'ctx')
- grad_kernel: float32 [31, 1536], replicated
- grad_gain: float32 [1536], replicated
- grad_down: float32 [64, 1536, 128], P('ctx', 'dp')
- grad_up: float32 [64, 128, 1536], P('ctx', None, 'dp')
The draws below stay inside these ranges and needn't reach their ends.
Inputs may be any that keep to these rules, and one draw needn't show every extreme that they name: On one device, the 16 segments' adapters lie at different ctx indices: the values lang_slot[segment_langs] // 2 differ. `lang_slot`: A permutation; slot s is kept by ctx index s // 2. `segment_lengths`: each row sums to 192; its largest entry is exactly 15.
All inputs are finite; a program needn't handle non-finite values.
Results may differ from the reference program's by a relative error of at most 0.0055.
Values may be sent and summed in bfloat16 or wider, within the bound.
No kernel may reach another device: no remote copies, remote signals or barrier semaphores. Data moves between devices by JAX's collectives and lax.ppermute only.
A program may use at most 64 MiB of HBM per device.

```python
import math
import jax
import jax.numpy as jnp
import numpy as np
from jax import lax

D = 1536
KER = 31
R = 128
LANG_DEV = 2
F_DEV = 192
SEG_DEV = 16
CAP = 15
LANG = 64
RECS = 16
FRAMES = 6144
N_CTX = 32


def shared_table(key):
    return jax.random.permutation(jax.random.fold_in(key, 101), LANG).astype(jnp.int32)


def draw_lang_slot(key, part):
    slot_of = shared_table(key)
    return slot_of


def draw_segment_langs(key, part):
    slot_of = shared_table(key)
    key = jax.random.fold_in(key, 7)
    lang_of_slot = jnp.argsort(slot_of, stable=True).astype(jnp.int32)
    score_key, pick_key = jax.random.split(key)
    scores = jax.random.randint(score_key, (RECS, N_CTX, N_CTX), 0, 1 << 20, dtype=jnp.int32) * N_CTX + jnp.arange(N_CTX, dtype=jnp.int32)
    owners = jnp.argsort(scores, axis=-1, stable=True)[..., :SEG_DEV].astype(jnp.int32)
    local_pick = jax.random.randint(pick_key, (RECS, N_CTX, SEG_DEV), 0, LANG_DEV, dtype=jnp.int32)
    slots = owners * LANG_DEV + local_pick
    return jnp.take(lang_of_slot, slots).astype(jnp.int32)


def block_scale(stream_key, extent, shards, least, largest):
    def one(axis_at, shards_of):
        steps = jax.random.uniform(jax.random.fold_in(jax.random.fold_in(stream_key, 6), axis_at), (shards_of,), jnp.float32, least / len(shards), largest / len(shards))
        return jnp.repeat(jnp.exp(steps), extent[axis_at] // shards_of).reshape((-1,) + (1,) * (len(extent) - axis_at - 1))

    gain = one(*shards[0])
    for cut in shards[1:]:
        gain = gain * one(*cut)
    return gain


def profile(count, total, reach, lean):
    loads = [(1 << 20) // math.isqrt(standing ** lean) + 1 for standing in range(2, count + 1)]
    surplus, holding = total - reach - (count - 1), [1] * (count - 1)
    while surplus > 0:
        free = [i for i in range(count - 1) if holding[i] < reach]
        pool, left = sum([loads[i] for i in free]), surplus
        for i in free:
            more = min(reach - holding[i], max(1, left * loads[i] // pool), surplus)
            holding[i] = holding[i] + more
            surplus = surplus - more
    return np.array([reach] + holding)


def ragged(rng, amount, total, bound, slope):
    if amount == 2:
        one = jax.random.randint(rng, (), max(1, total - bound), min(bound, total - 1) + 1)
        return jnp.stack([one, total - one])
    tallies = jnp.asarray(profile(amount, total, bound, slope), jnp.int32)
    twos = (amount - 1) // 2
    source_of, sink = tallies[1:1 + 2 * twos:2], tallies[2:2 + 2 * twos:2]
    margin = jnp.minimum(source_of - 1, bound - sink)
    moved = jax.random.randint(jax.random.fold_in(rng, 1), (twos,), 0, 1 << 20) % (margin + 1)
    tallies = tallies.at[1:1 + 2 * twos:2].set(source_of - moved).at[2:2 + 2 * twos:2].set(sink + moved)
    return tallies[jax.random.permutation(jax.random.fold_in(rng, 2), amount)]


def centred(rng, dims, scale, most, pieces=(), kind=jnp.bfloat16):
    values = jax.random.normal(rng, dims, jnp.float32) * scale
    if len(pieces) > 0:
        values = block_scale(rng, dims, pieces, -0.22, 0.18) * values
    return jnp.clip(values, min=-most, max=most).astype(kind)


def setup_inputs(seed: int = 0) -> dict:
    arg_keys = jax.random.split(jax.random.key(seed), 10)
    return {
        "inputs": centred(arg_keys[0], (RECS, FRAMES, D), 1.0, 6.0, ((0, 16), (1, 32))),
        "cotangent": centred(arg_keys[1], (RECS, FRAMES, D), 1.0, 6.0, ((0, 16), (1, 32))),
        "conv_kernel": centred(arg_keys[2], (KER, D), KER ** -0.5, 1.0, (), jnp.float32),
        "norm_gain": jnp.clip(1.0 + 0.1 * jax.random.normal(arg_keys[3], (D,), jnp.float32), 0.5, 1.5),
        "adapt_down": centred(arg_keys[4], (LANG, D, R), D ** -0.5, 0.15625, ((0, 32),)),
        "adapt_up": centred(arg_keys[5], (LANG, R, D), R ** -0.5, 0.5, ((0, 32),)),
        "segment_lengths": jax.vmap(lambda own: ragged(own, SEG_DEV, F_DEV, CAP, 2))(jax.random.split(arg_keys[6], RECS * N_CTX)).reshape((RECS, N_CTX, SEG_DEV)).astype(jnp.int32),
        "segment_langs": draw_segment_langs(jax.random.fold_in(arg_keys[9], 71), 0),
        "lang_slot": draw_lang_slot(jax.random.fold_in(arg_keys[9], 71), 0),
    }


def silu_slope(pre_act):
    sigmoid_val = jax.nn.sigmoid(pre_act)
    return sigmoid_val * (1.0 + pre_act * (1.0 - sigmoid_val))

def reference(inputs, cotangent, conv_kernel, norm_gain, adapt_down, adapt_up, segment_lengths, segment_langs, lang_slot):
    half_width = KER // 2
    frames_in = inputs.astype(jnp.float32)
    padded = jnp.pad(frames_in, ((0, 0), (half_width, half_width), (0, 0)))
    conv_out = jnp.zeros_like(frames_in)
    for offset in range(KER):
        conv_out = conv_out + conv_kernel[offset] * padded[:, offset:offset + FRAMES]
    summed = frames_in + conv_out
    inv_rms = lax.rsqrt(lax.optimization_barrier(jnp.mean(summed * summed, axis=-1, keepdims=True)) + 1e-06)
    normed = (summed * inv_rms * norm_gain).astype(jnp.bfloat16)
    seg_ends = jnp.cumsum(segment_lengths, axis=-1).astype(jnp.int32)
    seg_starts = (seg_ends - segment_lengths).astype(jnp.int32)
    offsets = (jnp.arange(N_CTX, dtype=jnp.int32) * F_DEV)[None, :, None]
    glob_starts = (seg_starts + offsets).reshape(-1).astype(jnp.int32)
    seg_slots = jnp.take(lang_slot, segment_langs.reshape(-1)).astype(jnp.int32)
    rec_ids = jnp.repeat(jnp.arange(RECS, dtype=jnp.int32), N_CTX * SEG_DEV)
    flat_lens = segment_lengths.reshape(-1).astype(jnp.int32)
    position = jnp.arange(CAP, dtype=jnp.int32)

    def one_segment(totals, segment):
        down_total, up_total = totals
        rec_id, start_at, length, slot_id = segment
        inside = position < length
        indices = jnp.clip(start_at + position, 0, FRAMES - 1).astype(jnp.int32)
        rows = jnp.where(inside[:, None], normed[rec_id][indices], jnp.zeros((), normed.dtype))
        grad_rows = jnp.where(inside[:, None], cotangent[rec_id][indices], jnp.zeros((), cotangent.dtype))
        down_w = adapt_down[slot_id]
        up_w = adapt_up[slot_id]
        pre_act = jnp.dot(rows, down_w, preferred_element_type=jnp.float32)
        activated = jax.nn.silu(pre_act).astype(jnp.bfloat16)
        branch = jnp.dot(activated, up_w, preferred_element_type=jnp.float32).astype(jnp.bfloat16)
        grad_act = jnp.dot(grad_rows, up_w.T, preferred_element_type=jnp.float32)
        grad_pre = (grad_act * silu_slope(pre_act)).astype(jnp.bfloat16)
        grad_normed = jnp.dot(grad_pre, down_w.T, preferred_element_type=jnp.float32).astype(jnp.bfloat16)
        down_total = down_total.at[slot_id].add(jnp.dot(rows.T, grad_pre, preferred_element_type=jnp.float32))
        up_total = up_total.at[slot_id].add(jnp.dot(activated.T, grad_rows, preferred_element_type=jnp.float32))
        return ((down_total, up_total), (branch, grad_normed))
    zero_grads = (jnp.zeros((LANG, D, R), jnp.float32), jnp.zeros((LANG, R, D), jnp.float32))
    (down_grad, up_grad), (branches, grad_normeds) = lax.scan(one_segment, zero_grads, (rec_ids, glob_starts, flat_lens, seg_slots))
    frame_local = jnp.arange(F_DEV, dtype=jnp.int32)
    seg_index = lax.optimization_barrier(jnp.sum((frame_local[None, None, :, None] >= seg_ends[:, :, None, :]).astype(jnp.int32), axis=-1)).astype(jnp.int32)
    start_of = jnp.take_along_axis(seg_starts, seg_index, axis=-1)
    within = (frame_local[None, None, :] - start_of).astype(jnp.int32)
    flat_seg = ((jnp.arange(RECS, dtype=jnp.int32)[:, None, None] * N_CTX + jnp.arange(N_CTX, dtype=jnp.int32)[None, :, None]) * SEG_DEV + seg_index).astype(jnp.int32)
    branch_frames = branches[flat_seg, within].reshape(RECS, FRAMES, D)
    grad_frames = grad_normeds[flat_seg, within].reshape(RECS, FRAMES, D).astype(jnp.float32)
    output = (summed + branch_frames.astype(jnp.float32)).astype(jnp.bfloat16)
    weighted = norm_gain * grad_frames
    inner_sum = lax.optimization_barrier(jnp.mean(weighted * summed, axis=-1, keepdims=True))
    grad_sum = cotangent.astype(jnp.float32) + inv_rms * weighted - summed * (inv_rms * inv_rms * inv_rms) * inner_sum
    grad_pad = jnp.pad(grad_sum, ((0, 0), (half_width, half_width), (0, 0)))
    grad_input = grad_sum
    for offset in range(KER):
        grad_input = grad_input + conv_kernel[offset] * grad_pad[:, 2 * half_width - offset:2 * half_width - offset + FRAMES]
    grad_scale = 1.0 / math.sqrt(RECS * FRAMES)
    grad_kernel = jnp.stack([lax.optimization_barrier(jnp.sum(grad_sum * padded[:, offset:offset + FRAMES], axis=(0, 1))) for offset in range(KER)]) * grad_scale
    grad_gain = lax.optimization_barrier(jnp.sum(grad_frames * summed * inv_rms, axis=(0, 1))) * grad_scale
    return (output, grad_input.astype(jnp.bfloat16), grad_kernel, grad_gain, down_grad * grad_scale, up_grad * grad_scale)
```

```python
import functools
import math

import jax
import jax.numpy as jnp
from jax import lax
from jax.experimental import pallas as pl
from jax.experimental.pallas import tpu as pltpu
from jax.sharding import PartitionSpec as P

BLOCK = 16
SEGMENTS = 16
EDGE = 16
LANES = 128
VMEM = pl.BlockSpec(memory_space=pltpu.VMEM)
SMEM = pl.BlockSpec(memory_space=pltpu.SMEM)
PARAMS = pltpu.CompilerParams(vmem_limit_bytes=40 * 1024 * 1024)
F32 = jnp.float32
BF16 = jnp.bfloat16


def call(body, outs, ins, scratch=()):
    return pl.pallas_call(
        body,
        out_shape=tuple(jax.ShapeDtypeStruct(shape, kind) for shape, kind in outs),
        in_specs=[SMEM if space == "s" else VMEM for space, _ in ins],
        out_specs=tuple(VMEM for _ in outs),
        scratch_shapes=[pltpu.VMEM(shape, kind) for shape, kind in scratch],
        compiler_params=PARAMS,
    )(*[array for _, array in ins])


def segments(numbers):
    start = jnp.int32(0)
    found = []
    for seg in range(SEGMENTS):
        slot = numbers[2 * SEGMENTS + numbers[SEGMENTS + seg]]
        end = start + numbers[seg]
        found.append((start, end, slot // 2, slot % 2))
        start = end
    return found


def frame_slots(found, shape, dim):
    frame = lax.broadcasted_iota(jnp.int32, shape, dim)
    slot = jnp.zeros(shape, jnp.int32)
    for start, end, keeper, _ in found:
        slot = jnp.where((frame >= start) & (frame < end), keeper * BLOCK - start + frame, slot)
    return slot


def scatter_matrix(found, rows, frames):
    slot = frame_slots(found, (1, frames), 1)
    row = lax.broadcasted_iota(jnp.int32, (rows, frames), 0)
    return jnp.where(row == slot, 1.0, 0.0).astype(BF16)


def gather_matrix(found, rows, frames):
    slot = frame_slots(found, (frames, LANES), 0)
    lane = lax.broadcasted_iota(jnp.int32, (frames, LANES), 1)
    parts = [jnp.where(lane + at == slot, 1.0, 0.0) for at in range(0, rows, LANES)]
    return jnp.concatenate(parts, axis=1).astype(BF16)


def shifted(cells, by):
    return cells if by == 0 else pltpu.roll(cells, cells.shape[0] - by, 0)


def send_cotangent(numbers, cot, send):
    found = segments(numbers)
    rows = send.shape[0]
    spread = scatter_matrix(found, rows, cot.shape[0])
    row = lax.broadcasted_iota(jnp.int32, (rows, LANES), 0)
    mark = jnp.zeros((rows, LANES), F32)
    for _, _, keeper, which in found:
        mark = jnp.where(row == keeper * BLOCK + BLOCK - 1, which.astype(F32), mark)
    moved = jnp.dot(spread, cot[...], preferred_element_type=F32)
    send[...] = moved.astype(BF16)
    send[:, :LANES] = (moved[:, :LANES] + mark).astype(BF16)


def conv_and_norm(numbers, left, own, right, taps, gain, send, summed, inv, cells, normed):
    frames, width = own.shape
    cells[:EDGE] = left[...].astype(F32)
    cells[EDGE : EDGE + frames] = own[...].astype(F32)
    cells[EDGE + frames :] = right[...].astype(F32)
    half = frames // 2

    def column(at, squares):
        lanes = pl.ds(pl.multiple_of(at * LANES, LANES), LANES)
        sums = []
        for part in range(2):
            block = cells[part * half : part * half + half + 2 * EDGE, lanes]
            total = block[EDGE : EDGE + half]
            for low in range(8):
                moved = shifted(block, low)
                for high in range(0, 32, 8):
                    if high + low > 0:
                        tap = taps[high + low - 1 : high + low, lanes]
                        total = total + tap * moved[high : high + half]
            summed[part * half : part * half + half, lanes] = total
            sums.append(total * total)
        return squares + jnp.concatenate(sums, axis=0)

    squares = lax.fori_loop(0, width // LANES, column, jnp.zeros((frames, LANES), F32))
    scale = lax.rsqrt(jnp.sum(squares, axis=1, keepdims=True) * (1.0 / width) + 1e-06)
    inv[...] = jnp.broadcast_to(scale, inv.shape)
    normed[...] = (summed[...] * scale * gain[...]).astype(BF16)
    spread = scatter_matrix(segments(numbers), send.shape[0], frames)
    send[...] = jnp.dot(spread, normed[...], preferred_element_type=F32).astype(BF16)


def keeper_back(rows_in, cot_in, down, up, back, pre_grad, act):
    rows, width = rows_in.shape
    units = down.shape[2]
    marks = cot_in[:, :units].astype(F32).reshape(rows // BLOCK, BLOCK, units)
    marks = jnp.broadcast_to(marks[:, BLOCK - 1 :, :], marks.shape).reshape(rows, units)
    keep = jnp.concatenate([1.0 - marks, marks], axis=1)
    both_down = jnp.concatenate([down[0], down[1]], axis=1)
    both_up = up[...].reshape(2 * units, width)
    pre = jnp.dot(rows_in[...], both_down, preferred_element_type=F32)
    slope_of = lax.dot_general(cot_in[...], both_up, (((1,), (1,)), ((), ())), preferred_element_type=F32)
    sig = jax.nn.sigmoid(pre)
    act[...] = (keep * (pre * sig)).astype(BF16)
    grads = (keep * (slope_of * (sig * (1.0 + pre * (1.0 - sig))))).astype(BF16)
    pre_grad[...] = grads
    back[...] = lax.dot_general(grads, both_down, (((1,), (1,)), ((), ())), preferred_element_type=F32).astype(BF16)


def keeper_branch(act, up, branch):
    both_up = up[...].reshape(act.shape[1], branch.shape[1])
    branch[...] = jnp.dot(act[...], both_up, preferred_element_type=F32).astype(BF16)


def keeper_grads(rows_in, cot_in, pre_grad, act, grads):
    parts, twice, units = grads.shape
    part = twice // 2
    down = lax.dot_general(rows_in[...], pre_grad[...], (((0,), (0,)), ((), ())), preferred_element_type=F32)
    up = lax.dot_general(cot_in[...], act[...], (((0,), (0,)), ((), ())), preferred_element_type=F32)
    for place, at in enumerate(turned(parts)):
        grads[place, :part] = down[at * part : at * part + part]
        grads[place, part:] = up[at * part : at * part + part]


def sum_gradients(
    numbers, back, cot, summed, inv, gain, left, own, right, total, edges, sums, cells, frames_grad
):
    frames, width = cot.shape
    gather = gather_matrix(segments(numbers), back.shape[0], frames)
    cells[:EDGE] = left[...].astype(F32)
    cells[EDGE : EDGE + frames] = own[...].astype(F32)
    cells[EDGE + frames :] = right[...].astype(F32)
    frames_grad[...] = jnp.dot(gather, back[...], preferred_element_type=F32)
    scale = inv[:, :1]
    inner = jnp.sum(gain[...] * frames_grad[...] * summed[...], axis=1, keepdims=True) * (1.0 / width)
    pull = scale * scale * scale * inner
    half = frames // 2

    def column(at, carry):
        lanes = pl.ds(pl.multiple_of(at * LANES, LANES), LANES)
        for part in range(2):
            span = slice(part * half, part * half + half)
            grad = frames_grad[span, lanes]
            base = summed[span, lanes]
            inverse = inv[span, :]
            gain_sum = jnp.sum(grad * base * inverse, axis=0, keepdims=True)
            whole = cot[span, lanes].astype(F32) + inverse * (gain[:, lanes] * grad) - base * pull[span]
            total[span, lanes] = whole
            block = cells[part * half : part * half + half + 2 * EDGE, lanes]
            found = [None] * 31
            for low in range(8):
                moved = shifted(block, low)
                for high in range(0, 32, 8):
                    if high + low > 0:
                        product = whole * moved[high : high + half]
                        found[high + low - 1] = jnp.sum(product, axis=0, keepdims=True)
            rows = jnp.concatenate(found + [gain_sum], axis=0)
            if part == 0:
                first = rows
            else:
                sums[:, lanes] = first + rows
        return carry

    lax.fori_loop(0, width // LANES, column, 0)
    edges[0] = total[:EDGE]
    edges[1] = total[frames - EDGE :]


def input_gradient(left, own, right, taps, out, cells):
    frames, width = own.shape
    cells[:EDGE] = left[...]
    cells[EDGE : EDGE + frames] = own[...]
    cells[EDGE + frames :] = right[...]
    half = frames // 2

    def column(at, carry):
        lanes = pl.ds(pl.multiple_of(at * LANES, LANES), LANES)
        for part in range(2):
            block = cells[part * half : part * half + half + 2 * EDGE, lanes]
            total = block[EDGE : EDGE + half]
            for low in range(8):
                moved = shifted(block, low)
                for high in range(0, 32, 8):
                    if high + low > 0:
                        tap = taps[31 - high - low : 32 - high - low, lanes]
                        total = total + tap * moved[high : high + half]
            out[part * half : part * half + half, lanes] = total.astype(BF16)
        return carry

    lax.fori_loop(0, width // LANES, column, 0)


def add_branch(numbers, back, summed, out):
    gather = gather_matrix(segments(numbers), back.shape[0], summed.shape[0])
    out[...] = (summed[...] + jnp.dot(gather, back[...], preferred_element_type=F32)).astype(BF16)


def place_grads(scale, kept, got, down, up):
    share, units = down.shape[1:]
    total = (kept[...] + got[...].astype(F32)) * scale
    for which in range(2):
        lanes = slice(which * units, which * units + units)
        down[which] = total[:share, lanes]
        up[which] = total[share:, lanes].T


def from_sides(head, tail, axis):
    count = lax.axis_size(axis)
    left = lax.ppermute(tail, axis, [(i, i + 1) for i in range(count - 1)])
    right = lax.ppermute(head, axis, [(i + 1, i) for i in range(count - 1)])
    return left, right


def turned(count):
    bits = count.bit_length() - 1
    return [sum(((at >> bit) & 1) << (bits - 1 - bit) for bit in range(bits)) for at in range(count)]


def halved(cells, axis, kind):
    count, me = lax.axis_size(axis), lax.axis_index(axis)
    step = 1
    while True:
        half = cells.shape[0] // 2
        upper = (me // step) % 2 == 1
        given = jnp.where(upper, cells[:half], cells[half:]).astype(kind)
        kept = jnp.where(upper, cells[half:], cells[:half])
        got = lax.ppermute(given, axis, [(i, i ^ step) for i in range(count)])
        step *= 2
        if step == count:
            return kept, got
        cells = kept + got.astype(cells.dtype)


def quartered(cells, axis):
    count, me = lax.axis_size(axis), lax.axis_index(axis)
    unit = count // 4
    while unit > 0:
        part = cells.shape[0] // 4
        blocks = [cells[at * part : at * part + part] for at in range(4)]
        mine = (me // unit) % 4

        def block(turn):
            place = mine ^ turn
            low = jnp.where(place == 0, blocks[0], blocks[1])
            return jnp.where(place < 2, low, jnp.where(place == 2, blocks[2], blocks[3]))

        moved = [lax.ppermute(block(turn), axis, [(i, i ^ (turn * unit)) for i in range(count)]) for turn in (1, 2, 3)]
        cells = (block(0) + moved[0]) + (moved[1] + moved[2])
        unit //= 4
    return cells


def swap(cells, axis):
    return lax.all_to_all(cells, axis, split_axis=0, concat_axis=0, tiled=True)


def spread_rows(rows, axis):
    count = lax.axis_size(axis)
    return swap(jnp.broadcast_to(rows[None], (count,) + rows.shape), axis)


def local(
    inputs, cotangent, conv_kernel, norm_gain, adapt_down, adapt_up, segment_lengths, segment_langs, lang_slot
):
    frames, width = inputs.shape[1:]
    units = adapt_down.shape[2]
    dp, ctx = lax.axis_size("dp"), lax.axis_size("ctx")
    rows = ctx * BLOCK
    own, cot = inputs[0], cotangent[0]
    gain = norm_gain.reshape(1, width)
    numbers = jnp.concatenate([segment_lengths.reshape(-1), segment_langs.reshape(-1), lang_slot])
    where = [("s", numbers)]

    left, right = from_sides(own[:EDGE], own[frames - EDGE :], "ctx")
    (send_cot,) = call(send_cotangent, [((rows, width), BF16)], where + [("v", cot)])
    left, right, send_cot = lax.optimization_barrier((left, right, send_cot))
    got_cot = swap(send_cot, "ctx")
    send_rows, summed, inv = call(
        conv_and_norm,
        [((rows, width), BF16), ((frames, width), F32), ((frames, LANES), F32)],
        where + [("v", left), ("v", own), ("v", right), ("v", conv_kernel), ("v", gain)],
        [((frames + 2 * EDGE, width), F32), ((frames, width), BF16)],
    )
    got_rows = swap(send_rows, "ctx")
    back, pre_grad, act = call(
        keeper_back,
        [((rows, width), BF16), ((rows, 2 * units), BF16), ((rows, 2 * units), BF16)],
        [("v", got_rows), ("v", got_cot), ("v", adapt_down), ("v", adapt_up)],
    )
    grad_back = swap(back, "ctx")
    (branch,) = call(keeper_branch, [((rows, width), BF16)], [("v", act), ("v", adapt_up)])
    (parts,) = call(
        keeper_grads,
        [((dp, 2 * (width // dp), 2 * units), F32)],
        [("v", got_rows), ("v", got_cot), ("v", pre_grad), ("v", act)],
    )
    kept, got = halved(parts, "dp", BF16)
    grad_back, branch = lax.optimization_barrier((grad_back, branch))
    branch_back = swap(branch, "ctx")
    total, edges, sums = call(
        sum_gradients,
        [((frames, width), F32), ((2, EDGE, width), F32), ((32, width), F32)],
        where
        + [("v", grad_back), ("v", cot), ("v", summed), ("v", inv), ("v", gain)]
        + [("v", left), ("v", own), ("v", right)],
        [((frames + 2 * EDGE, width), F32), ((frames, width), F32)],
    )
    grad_left, grad_right = from_sides(edges[0], edges[1], "ctx")
    mine, branch_back = lax.optimization_barrier((quartered(sums, "dp"), branch_back))
    mine = jnp.sum(spread_rows(mine, "ctx"), axis=0)
    grad_scale = 1.0 / math.sqrt(dp * ctx * frames)
    (grad_input,) = call(
        input_gradient,
        [((frames, width), BF16)],
        [("v", grad_left), ("v", total), ("v", grad_right), ("v", conv_kernel)],
        [((frames + 2 * EDGE, width), F32)],
    )
    (output,) = call(add_branch, [((frames, width), BF16)], where + [("v", branch_back), ("v", summed)])
    mine, grad_input, output = lax.optimization_barrier((mine, grad_input, output))
    reduced = spread_rows(mine * grad_scale, "dp").reshape(32, width)
    share = width // dp
    grad_down, grad_up = call(
        functools.partial(place_grads, grad_scale),
        [((2, share, units), F32), ((2, units, share), F32)],
        [("v", kept[0]), ("v", got[0])],
    )
    return output[None], grad_input[None], reduced[:31], reduced[31], grad_down, grad_up


def solution(mesh):
    in_specs = (
        P("dp", "ctx", None),
        P("dp", "ctx", None),
        P(),
        P(),
        P("ctx", None, None),
        P("ctx", None, None),
        P("dp", "ctx", None),
        P("dp", "ctx", None),
        P(),
    )
    out_specs = (
        P("dp", "ctx", None),
        P("dp", "ctx", None),
        P(),
        P(),
        P("ctx", "dp", None),
        P("ctx", None, "dp"),
    )
    return jax.shard_map(local, mesh=mesh, in_specs=in_specs, out_specs=out_specs, check_vma=False)
```

```python
import functools
import math

import jax
import jax.numpy as jnp
from jax import lax
from jax.experimental import pallas as pl
from jax.experimental.pallas import tpu as pltpu
from jax.sharding import PartitionSpec as P

BLOCK = 16
SEGMENTS = 16
EDGE = 16
LANES = 128
VMEM = pl.BlockSpec(memory_space=pltpu.VMEM)
SMEM = pl.BlockSpec(memory_space=pltpu.SMEM)
PARAMS = pltpu.CompilerParams(vmem_limit_bytes=40 * 1024 * 1024)
F32 = jnp.float32
BF16 = jnp.bfloat16


def call(body, outs, ins, scratch=(), moves=None):
    cost = None if moves is None else pl.CostEstimate(flops=0, transcendentals=0, bytes_accessed=moves)
    return pl.pallas_call(
        body,
        cost_estimate=cost,
        out_shape=tuple(jax.ShapeDtypeStruct(shape, kind) for shape, kind in outs),
        in_specs=[SMEM if space == "s" else VMEM for space, _ in ins],
        out_specs=tuple(VMEM for _ in outs),
        scratch_shapes=[pltpu.VMEM(shape, kind) for shape, kind in scratch],
        compiler_params=PARAMS,
    )(*[array for _, array in ins])


def segments(numbers):
    start = jnp.int32(0)
    found = []
    for seg in range(SEGMENTS):
        slot = numbers[2 * SEGMENTS + numbers[SEGMENTS + seg]]
        end = start + numbers[seg]
        found.append((start, end, slot // 2, slot % 2))
        start = end
    return found


def frame_slots(found, shape, dim):
    frame = lax.broadcasted_iota(jnp.int32, shape, dim)
    slot = jnp.zeros(shape, jnp.int32)
    for start, end, keeper, _ in found:
        slot = jnp.where((frame >= start) & (frame < end), keeper * BLOCK - start + frame, slot)
    return slot


def scatter_matrix(found, rows, frames):
    slot = frame_slots(found, (1, frames), 1)
    row = lax.broadcasted_iota(jnp.int32, (rows, frames), 0)
    return jnp.where(row == slot, 1.0, 0.0).astype(BF16)


def gather_matrix(found, rows, frames):
    slot = frame_slots(found, (frames, LANES), 0)
    lane = lax.broadcasted_iota(jnp.int32, (frames, LANES), 1)
    parts = [jnp.where(lane + at == slot, 1.0, 0.0) for at in range(0, rows, LANES)]
    return jnp.concatenate(parts, axis=1).astype(BF16)


def shifted(cells, by):
    return cells if by == 0 else pltpu.roll(cells, cells.shape[0] - by, 0)


def send_cotangent(numbers, cot, send):
    found = segments(numbers)
    rows = send.shape[0]
    spread = scatter_matrix(found, rows, cot.shape[0])
    row = lax.broadcasted_iota(jnp.int32, (rows, LANES), 0)
    mark = jnp.zeros((rows, LANES), F32)
    for _, _, keeper, which in found:
        mark = jnp.where(row == keeper * BLOCK + BLOCK - 1, which.astype(F32), mark)
    moved = jnp.dot(spread, cot[...], preferred_element_type=F32)
    send[...] = moved.astype(BF16)
    send[:, :LANES] = (moved[:, :LANES] + mark).astype(BF16)


def conv_and_norm(numbers, left, own, right, taps, gain, send, summed, inv, cells, normed):
    frames, width = own.shape
    cells[:EDGE] = left[...].astype(F32)
    cells[EDGE : EDGE + frames] = own[...].astype(F32)
    cells[EDGE + frames :] = right[...].astype(F32)
    half = frames // 2

    def column(at, squares):
        lanes = pl.ds(pl.multiple_of(at * LANES, LANES), LANES)
        sums = []
        for part in range(2):
            block = cells[part * half : part * half + half + 2 * EDGE, lanes]
            total = block[EDGE : EDGE + half]
            for low in range(8):
                moved = shifted(block, low)
                for high in range(0, 32, 8):
                    if high + low > 0:
                        tap = taps[high + low - 1 : high + low, lanes]
                        total = total + tap * moved[high : high + half]
            summed[part * half : part * half + half, lanes] = total
            sums.append(total * total)
        return squares + jnp.concatenate(sums, axis=0)

    squares = lax.fori_loop(0, width // LANES, column, jnp.zeros((frames, LANES), F32))
    scale = lax.rsqrt(jnp.sum(squares, axis=1, keepdims=True) * (1.0 / width) + 1e-06)
    inv[...] = jnp.broadcast_to(scale, inv.shape)
    normed[...] = (summed[...] * scale * gain[...]).astype(BF16)
    spread = scatter_matrix(segments(numbers), send.shape[0], frames)
    send[...] = jnp.dot(spread, normed[...], preferred_element_type=F32).astype(BF16)


def keeper_back(rows_in, cot_in, down, up, back, pre_grad, act):
    rows, width = rows_in.shape
    units = down.shape[2]
    marks = cot_in[:, :units].astype(F32).reshape(rows // BLOCK, BLOCK, units)
    marks = jnp.broadcast_to(marks[:, BLOCK - 1 :, :], marks.shape).reshape(rows, units)
    keep = jnp.concatenate([1.0 - marks, marks], axis=1)
    both_down = jnp.concatenate([down[0], down[1]], axis=1)
    both_up = up[...].reshape(2 * units, width)
    pre = jnp.dot(rows_in[...], both_down, preferred_element_type=F32)
    slope_of = lax.dot_general(cot_in[...], both_up, (((1,), (1,)), ((), ())), preferred_element_type=F32)
    sig = jax.nn.sigmoid(pre)
    act[...] = (keep * (pre * sig)).astype(BF16)
    grads = (keep * (slope_of * (sig * (1.0 + pre * (1.0 - sig))))).astype(BF16)
    pre_grad[...] = grads
    back[...] = lax.dot_general(grads, both_down, (((1,), (1,)), ((), ())), preferred_element_type=F32).astype(BF16)


def keeper_branch(act, up, branch):
    both_up = up[...].reshape(act.shape[1], branch.shape[1])
    branch[...] = jnp.dot(act[...], both_up, preferred_element_type=F32).astype(BF16)


def keeper_grads(place, rows_in, cot_in, pre_grad, act, kept, given, down, up):
    parts, twice, _ = kept.shape
    part = twice // 2
    core = place[0] % 2
    down[...] = lax.dot_general(rows_in[...], pre_grad[...], (((0,), (0,)), ((), ())), preferred_element_type=F32)
    up[...] = lax.dot_general(cot_in[...], act[...], (((0,), (0,)), ((), ())), preferred_element_type=F32)
    for at in range(parts):
        near = pl.ds(pl.multiple_of((2 * at + core) * part, part), part)
        far = pl.ds(pl.multiple_of((2 * at + 1 - core) * part, part), part)
        kept[at, :part] = down[near]
        kept[at, part:] = up[near]
        given[at, :part] = down[far].astype(BF16)
        given[at, part:] = up[far].astype(BF16)


def share_grads(place, kept, got, own, *given):
    chip = place[0] // 2
    for turn, out in enumerate((own,) + given):
        for high in range(out.shape[0]):
            at = 4 * high + ((chip % 4) ^ turn)
            out[high] = (kept[at] + got[at].astype(F32)).astype(out.dtype)


def pair_grads(place, own, first, second, third, kept, given):
    high = place[0] // 8
    for at, out in ((high, kept), (1 - high, given)):
        total = own[at] + first[at].astype(F32) + second[at].astype(F32) + third[at].astype(F32)
        out[...] = total.astype(out.dtype)


def sum_gradients(
    numbers, place, back, cot, summed, inv, gain, left, own, right, total, edges, *rest
):
    *quarters, sums, cells, frames_grad = rest
    frames, width = cot.shape
    gather = gather_matrix(segments(numbers), back.shape[0], frames)
    cells[:EDGE] = left[...].astype(F32)
    cells[EDGE : EDGE + frames] = own[...].astype(F32)
    cells[EDGE + frames :] = right[...].astype(F32)
    frames_grad[...] = jnp.dot(gather, back[...], preferred_element_type=F32)
    scale = inv[:, :1]
    inner = jnp.sum(gain[...] * frames_grad[...] * summed[...], axis=1, keepdims=True) * (1.0 / width)
    pull = scale * scale * scale * inner
    half = frames // 2

    def column(at, carry):
        lanes = pl.ds(pl.multiple_of(at * LANES, LANES), LANES)
        for part in range(2):
            span = slice(part * half, part * half + half)
            grad = frames_grad[span, lanes]
            base = summed[span, lanes]
            inverse = inv[span, :]
            gain_sum = jnp.sum(grad * base * inverse, axis=0, keepdims=True)
            whole = cot[span, lanes].astype(F32) + inverse * (gain[:, lanes] * grad) - base * pull[span]
            total[span, lanes] = whole
            block = cells[part * half : part * half + half + 2 * EDGE, lanes]
            found = [None] * 31
            for low in range(8):
                moved = shifted(block, low)
                for high in range(0, 32, 8):
                    if high + low > 0:
                        product = whole * moved[high : high + half]
                        found[high + low - 1] = jnp.sum(product, axis=0, keepdims=True)
            rows = jnp.concatenate(found + [gain_sum], axis=0)
            if part == 0:
                first = rows
            else:
                sums[:, lanes] = first + rows
        return carry

    lax.fori_loop(0, width // LANES, column, 0)
    edges[0] = total[:EDGE]
    edges[1] = total[frames - EDGE :]
    for turn, out in enumerate(quarters):
        at = (place[0] // 4) ^ turn
        out[...] = sums[pl.ds(pl.multiple_of(at * 8, 8), 8)]


def input_gradient(left, own, right, taps, out, cells):
    frames, width = own.shape
    cells[:EDGE] = left[...]
    cells[EDGE : EDGE + frames] = own[...]
    cells[EDGE + frames :] = right[...]
    half = frames // 2

    def column(at, carry):
        lanes = pl.ds(pl.multiple_of(at * LANES, LANES), LANES)
        for part in range(2):
            block = cells[part * half : part * half + half + 2 * EDGE, lanes]
            total = block[EDGE : EDGE + half]
            for low in range(8):
                moved = shifted(block, low)
                for high in range(0, 32, 8):
                    if high + low > 0:
                        tap = taps[31 - high - low : 32 - high - low, lanes]
                        total = total + tap * moved[high : high + half]
            out[part * half : part * half + half, lanes] = total.astype(BF16)
        return carry

    lax.fori_loop(0, width // LANES, column, 0)


def add_branch(numbers, back, summed, out):
    gather = gather_matrix(segments(numbers), back.shape[0], summed.shape[0])
    out[...] = (summed[...] + jnp.dot(gather, back[...], preferred_element_type=F32)).astype(BF16)


def place_grads(scale, kept, got, down, up):
    share, units = down.shape[1:]
    total = (kept[...] + got[...].astype(F32)) * scale
    for which in range(2):
        lanes = slice(which * units, which * units + units)
        down[which] = total[:share, lanes]
        up[which] = total[share:, lanes]


def from_sides(head, tail, axis):
    count = lax.axis_size(axis)
    left = lax.ppermute(tail, axis, [(i, i + 1) for i in range(count - 1)])
    right = lax.ppermute(head, axis, [(i + 1, i) for i in range(count - 1)])
    return left, right


def exchanged(blocks, axis, unit):
    count = lax.axis_size(axis)
    return [
        lax.ppermute(block, axis, [(i, i ^ (turn * unit)) for i in range(count)])
        for turn, block in enumerate(blocks[1:], 1)
    ]


def quarter(cells, mine):
    part = cells.shape[0] // 4
    blocks = [cells[at * part : at * part + part] for at in range(4)]
    places = [mine ^ turn for turn in range(4)]
    return [
        jnp.where(at < 2, jnp.where(at == 0, blocks[0], blocks[1]), jnp.where(at == 2, blocks[2], blocks[3]))
        for at in places
    ]


def swap(cells, axis):
    return lax.all_to_all(cells, axis, split_axis=0, concat_axis=0, tiled=True)


def spread_rows(rows, axis):
    count = lax.axis_size(axis)
    return swap(jnp.broadcast_to(rows[None], (count,) + rows.shape), axis)


def local(
    inputs, cotangent, conv_kernel, norm_gain, adapt_down, adapt_up, segment_lengths, segment_langs, lang_slot
):
    frames, width = inputs.shape[1:]
    units = adapt_down.shape[2]
    dp, ctx = lax.axis_size("dp"), lax.axis_size("ctx")
    rows = ctx * BLOCK
    own, cot = inputs[0], cotangent[0]
    gain = norm_gain.reshape(1, width)
    numbers = jnp.concatenate([segment_lengths.reshape(-1), segment_langs.reshape(-1), lang_slot])
    where = [("s", numbers)]

    left, right = from_sides(own[:EDGE], own[frames - EDGE :], "ctx")
    (send_cot,) = call(send_cotangent, [((rows, width), BF16)], where + [("v", cot)])
    left, right, send_cot = lax.optimization_barrier((left, right, send_cot))
    got_cot = swap(send_cot, "ctx")
    send_rows, summed, inv = call(
        conv_and_norm,
        [((rows, width), BF16), ((frames, width), F32), ((frames, LANES), F32)],
        where + [("v", left), ("v", own), ("v", right), ("v", conv_kernel), ("v", gain)],
        [((frames + 2 * EDGE, width), F32), ((frames, width), BF16)],
        moves=24_000_000,
    )
    got_rows = swap(send_rows, "ctx")
    back, pre_grad, act = call(
        keeper_back,
        [((rows, width), BF16), ((rows, 2 * units), BF16), ((rows, 2 * units), BF16)],
        [("v", got_rows), ("v", got_cot), ("v", adapt_down), ("v", adapt_up)],
    )
    grad_back = swap(back, "ctx")
    (branch,) = call(keeper_branch, [((rows, width), BF16)], [("v", act), ("v", adapt_up)])
    share = width // dp
    place = ("s", lax.axis_index("dp").astype(jnp.int32).reshape(1))
    kept, given = call(
        keeper_grads,
        [((dp // 2, 2 * share, 2 * units), F32), ((dp // 2, 2 * share, 2 * units), BF16)],
        [place, ("v", got_rows), ("v", got_cot), ("v", pre_grad), ("v", act)],
        [((width, 2 * units), F32), ((width, 2 * units), F32)],
    )
    (got,) = exchanged([kept, given], "dp", 1)
    grad_scale = 1.0 / math.sqrt(dp * ctx * frames)
    piece = (2 * share, 2 * units)
    chips = call(
        share_grads,
        [((2,) + piece, F32)] + [((2,) + piece, BF16)] * 3,
        [place, ("v", kept), ("v", got)],
    )
    got = exchanged(chips, "dp", 2)
    kept, given = call(
        pair_grads, [(piece, F32), (piece, BF16)], [place, ("v", chips[0])] + [("v", part) for part in got]
    )
    (got,) = exchanged([kept, given], "dp", 8)
    grad_down, grad_up = call(
        functools.partial(place_grads, grad_scale), [((2, share, units), F32)] * 2, [("v", kept), ("v", got)]
    )
    grad_back, branch, grad_down, grad_up = lax.optimization_barrier((grad_back, branch, grad_down, grad_up))
    branch_back = swap(branch, "ctx")
    total, edges, *sums = call(
        sum_gradients,
        [((frames, width), F32), ((2, EDGE, width), F32)] + [((8, width), F32)] * 4,
        where
        + [place]
        + [("v", grad_back), ("v", cot), ("v", summed), ("v", inv), ("v", gain)]
        + [("v", left), ("v", own), ("v", right)],
        [((32, width), F32), ((frames + 2 * EDGE, width), F32), ((frames, width), F32)],
    )
    grad_left, grad_right = from_sides(edges[0], edges[1], "ctx")
    me = lax.axis_index("dp")
    mine = sums[0] + sum(exchanged(sums, "dp", 4))
    sums = quarter(mine, me % 4)
    mine = sums[0] + sum(exchanged(sums, "dp", 1))
    mine, branch_back = lax.optimization_barrier((mine, branch_back))
    mine = jnp.sum(spread_rows(mine, "ctx"), axis=0)
    (grad_input,) = call(
        input_gradient,
        [((frames, width), BF16)],
        [("v", grad_left), ("v", total), ("v", grad_right), ("v", conv_kernel)],
        [((frames + 2 * EDGE, width), F32)],
    )
    (output,) = call(add_branch, [((frames, width), BF16)], where + [("v", branch_back), ("v", summed)])
    mine, grad_input = lax.optimization_barrier((mine, grad_input))
    reduced = spread_rows(mine * grad_scale, "dp").reshape(32, width)
    return output[None], grad_input[None], reduced[:31], reduced[31], grad_down, jnp.transpose(grad_up, (0, 2, 1))


def solution(mesh):
    in_specs = (
        P("dp", "ctx", None),
        P("dp", "ctx", None),
        P(),
        P(),
        P("ctx", None, None),
        P("ctx", None, None),
        P("dp", "ctx", None),
        P("dp", "ctx", None),
        P(),
    )
    out_specs = (
        P("dp", "ctx", None),
        P("dp", "ctx", None),
        P(),
        P(),
        P("ctx", "dp", None),
        P("ctx", None, "dp"),
    )
    return jax.shard_map(local, mesh=mesh, in_specs=in_specs, out_specs=out_specs, check_vma=False)
```

```python
import functools
import math

import jax
import jax.numpy as jnp
from jax import lax
from jax.experimental import pallas as pl
from jax.experimental.pallas import tpu as pltpu
from jax.sharding import PartitionSpec as P

BLOCK = 16
SEGMENTS = 16
EDGE = 16
LANES = 128
VMEM = pl.BlockSpec(memory_space=pltpu.VMEM)
SMEM = pl.BlockSpec(memory_space=pltpu.SMEM)
PARAMS = pltpu.CompilerParams(vmem_limit_bytes=40 * 1024 * 1024)
F32 = jnp.float32
BF16 = jnp.bfloat16


def call(body, outs, ins, scratch=()):
    return pl.pallas_call(
        body,
        out_shape=tuple(jax.ShapeDtypeStruct(shape, kind) for shape, kind in outs),
        in_specs=[SMEM if space == "s" else VMEM for space, _ in ins],
        out_specs=tuple(VMEM for _ in outs),
        scratch_shapes=[pltpu.VMEM(shape, kind) for shape, kind in scratch],
        compiler_params=PARAMS,
    )(*[array for _, array in ins])


def segments(numbers):
    start = jnp.int32(0)
    found = []
    for seg in range(SEGMENTS):
        slot = numbers[2 * SEGMENTS + numbers[SEGMENTS + seg]]
        end = start + numbers[seg]
        found.append((start, end, slot // 2, slot % 2))
        start = end
    return found


def frame_slots(found, shape, dim):
    frame = lax.broadcasted_iota(jnp.int32, shape, dim)
    slot = jnp.zeros(shape, jnp.int32)
    for start, end, keeper, _ in found:
        slot = jnp.where((frame >= start) & (frame < end), keeper * BLOCK - start + frame, slot)
    return slot


def scatter_matrix(found, rows, frames):
    slot = frame_slots(found, (1, frames), 1)
    row = lax.broadcasted_iota(jnp.int32, (rows, frames), 0)
    return jnp.where(row == slot, 1.0, 0.0).astype(BF16)


def gather_matrix(found, rows, frames):
    slot = frame_slots(found, (frames, LANES), 0)
    lane = lax.broadcasted_iota(jnp.int32, (frames, LANES), 1)
    parts = [jnp.where(lane + at == slot, 1.0, 0.0) for at in range(0, rows, LANES)]
    return jnp.concatenate(parts, axis=1).astype(BF16)


def shifted(cells, by):
    return cells if by == 0 else pltpu.roll(cells, cells.shape[0] - by, 0)


def conv_and_norm(numbers, left, own, right, cot, taps, gain, send, summed, inv, cells, normed):
    frames, width = own.shape
    rows = send.shape[0] * BLOCK
    blocks = (send.shape[0], BLOCK, width)
    found = segments(numbers)
    spread = scatter_matrix(found, rows, frames)
    row = lax.broadcasted_iota(jnp.int32, (rows, LANES), 0)
    mark = jnp.zeros((rows, LANES), F32)
    for _, _, keeper, which in found:
        mark = jnp.where(row == keeper * BLOCK + BLOCK - 1, which.astype(F32), mark)
    moved = jnp.dot(spread, cot[...], preferred_element_type=F32)
    moved = jnp.concatenate([moved[:, :LANES] + mark, moved[:, LANES:]], axis=1)
    send[:, BLOCK:] = moved.astype(BF16).reshape(blocks)
    cells[:EDGE] = left[...].astype(F32)
    cells[EDGE : EDGE + frames] = own[...].astype(F32)
    cells[EDGE + frames :] = right[...].astype(F32)
    half = frames // 2

    def column(at, squares):
        lanes = pl.ds(pl.multiple_of(at * LANES, LANES), LANES)
        sums = []
        for part in range(2):
            block = cells[part * half : part * half + half + 2 * EDGE, lanes]
            total = block[EDGE : EDGE + half]
            for low in range(8):
                moved = shifted(block, low)
                for high in range(0, 32, 8):
                    if high + low > 0:
                        tap = taps[high + low - 1 : high + low, lanes]
                        total = total + tap * moved[high : high + half]
            summed[part * half : part * half + half, lanes] = total
            sums.append(total * total)
        return squares + jnp.concatenate(sums, axis=0)

    squares = lax.fori_loop(0, width // LANES, column, jnp.zeros((frames, LANES), F32))
    scale = lax.rsqrt(jnp.sum(squares, axis=1, keepdims=True) * (1.0 / width) + 1e-06)
    inv[...] = jnp.broadcast_to(scale, inv.shape)
    normed[...] = (summed[...] * scale * gain[...]).astype(BF16)
    send[:, :BLOCK] = jnp.dot(spread, normed[...], preferred_element_type=F32).astype(BF16).reshape(blocks)


def received(got):
    shape = (got.shape[0] * BLOCK, got.shape[2])
    return got[:, :BLOCK].reshape(shape), got[:, BLOCK:].reshape(shape)


def keeper_back(got, down, up, back, pre_grad, act):
    rows_in, cot_in = received(got)
    rows, width = rows_in.shape
    units = down.shape[2]
    marks = cot_in[:, :units].astype(F32).reshape(rows // BLOCK, BLOCK, units)
    marks = jnp.broadcast_to(marks[:, BLOCK - 1 :, :], marks.shape).reshape(rows, units)
    keep = jnp.concatenate([1.0 - marks, marks], axis=1)
    both_down = jnp.concatenate([down[0], down[1]], axis=1)
    both_up = up[...].reshape(2 * units, width)
    pre = jnp.dot(rows_in, both_down, preferred_element_type=F32)
    slope_of = lax.dot_general(cot_in, both_up, (((1,), (1,)), ((), ())), preferred_element_type=F32)
    sig = jax.nn.sigmoid(pre)
    act[...] = (keep * (pre * sig)).astype(BF16)
    grads = (keep * (slope_of * (sig * (1.0 + pre * (1.0 - sig))))).astype(BF16)
    pre_grad[...] = grads
    back[...] = lax.dot_general(grads, both_down, (((1,), (1,)), ((), ())), preferred_element_type=F32).astype(BF16)


def sum_last_rows(back, out):
    row = lax.broadcasted_iota(jnp.int32, (out.shape[0], back.shape[0]), 1)
    last = jnp.where(row % BLOCK == BLOCK - 1, 1.0, 0.0).astype(BF16)
    out[...] = jnp.dot(last, back[...], preferred_element_type=F32)


def keeper_grads(place, got, pre_grad, act, kept, given, down, up):
    parts, twice, _ = kept.shape
    part = twice // 2
    core = place[0] % 2
    rows_in, cot_in = received(got)
    down[...] = lax.dot_general(rows_in, pre_grad[...], (((0,), (0,)), ((), ())), preferred_element_type=F32)
    up[...] = lax.dot_general(cot_in, act[...], (((0,), (0,)), ((), ())), preferred_element_type=F32)
    for at in range(parts):
        near = pl.ds(pl.multiple_of((2 * at + core) * part, part), part)
        far = pl.ds(pl.multiple_of((2 * at + 1 - core) * part, part), part)
        kept[at, :part] = down[near]
        kept[at, part:] = up[near]
        given[at, :part] = down[far].astype(BF16)
        given[at, part:] = up[far].astype(BF16)


def share_grads(place, kept, got, own, *given):
    chip = place[0] // 2
    for turn, out in enumerate((own,) + given):
        for high in range(out.shape[0]):
            at = 4 * high + ((chip % 4) ^ turn)
            out[high] = (kept[at] + got[at].astype(F32)).astype(out.dtype)


def pair_grads(place, own, first, second, third, kept, given):
    high = place[0] // 8
    for at, out in ((high, kept), (1 - high, given)):
        total = own[at] + first[at].astype(F32) + second[at].astype(F32) + third[at].astype(F32)
        out[...] = total.astype(out.dtype)


def sum_gradients(
    numbers, back, cot, summed, inv, gain, left, own, right, act, up, total, edges, branch, sums, cells, frames_grad
):
    frames, width = cot.shape
    gather = gather_matrix(segments(numbers), back.shape[0], frames)
    cells[:EDGE] = left[...].astype(F32)
    cells[EDGE : EDGE + frames] = own[...].astype(F32)
    cells[EDGE + frames :] = right[...].astype(F32)
    frames_grad[...] = jnp.dot(gather, back[...], preferred_element_type=F32)
    scale = inv[:, :1]
    inner = jnp.sum(gain[...] * frames_grad[...] * summed[...], axis=1, keepdims=True) * (1.0 / width)
    pull = scale * scale * scale * inner
    half = frames // 2

    def column(at, carry):
        lanes = pl.ds(pl.multiple_of(at * LANES, LANES), LANES)
        for part in range(2):
            span = slice(part * half, part * half + half)
            grad = frames_grad[span, lanes]
            base = summed[span, lanes]
            inverse = inv[span, :]
            gain_sum = jnp.sum(grad * base * inverse, axis=0, keepdims=True)
            whole = cot[span, lanes].astype(F32) + inverse * (gain[:, lanes] * grad) - base * pull[span]
            total[span, lanes] = whole
            block = cells[part * half : part * half + half + 2 * EDGE, lanes]
            found = [None] * 31
            for low in range(8):
                moved = shifted(block, low)
                for high in range(0, 32, 8):
                    if high + low > 0:
                        product = whole * moved[high : high + half]
                        found[high + low - 1] = jnp.sum(product, axis=0, keepdims=True)
            rows = jnp.concatenate(found + [gain_sum], axis=0)
            if part == 0:
                first = rows
            else:
                sums[:, lanes] = first + rows
        return carry

    lax.fori_loop(0, width // LANES, column, 0)
    edges[0] = total[:EDGE]
    edges[1] = total[frames - EDGE :]
    both_up = up[...].reshape(act.shape[1], width)
    row = lax.broadcasted_iota(jnp.int32, (branch.shape[0], sums.shape[0]), 0)
    block = lax.broadcasted_iota(jnp.int32, (branch.shape[0], sums.shape[0]), 1)
    last = jnp.where(row == block * BLOCK + BLOCK - 1, 1.0, 0.0).astype(BF16)
    outputs = jnp.dot(act[...], both_up, preferred_element_type=F32)
    outputs = outputs + jnp.dot(last, sums[...].astype(BF16), preferred_element_type=F32)
    branch[...] = outputs.astype(BF16)


def input_gradient(left, own, right, taps, out, cells):
    frames, width = own.shape
    cells[:EDGE] = left[...]
    cells[EDGE : EDGE + frames] = own[...]
    cells[EDGE + frames :] = right[...]
    half = frames // 2

    def column(at, carry):
        lanes = pl.ds(pl.multiple_of(at * LANES, LANES), LANES)
        for part in range(2):
            block = cells[part * half : part * half + half + 2 * EDGE, lanes]
            total = block[EDGE : EDGE + half]
            for low in range(8):
                moved = shifted(block, low)
                for high in range(0, 32, 8):
                    if high + low > 0:
                        tap = taps[31 - high - low : 32 - high - low, lanes]
                        total = total + tap * moved[high : high + half]
            out[part * half : part * half + half, lanes] = total.astype(BF16)
        return carry

    lax.fori_loop(0, width // LANES, column, 0)


def add_branch(numbers, back, summed, out):
    gather = gather_matrix(segments(numbers), back.shape[0], summed.shape[0])
    out[...] = (summed[...] + jnp.dot(gather, back[...], preferred_element_type=F32)).astype(BF16)


def place_grads(scale, kept, got, down, up):
    share, units = down.shape[1:]
    total = (kept[...] + got[...].astype(F32)) * scale
    for which in range(2):
        lanes = slice(which * units, which * units + units)
        down[which] = total[:share, lanes]
        up[which] = total[share:, lanes]


def from_sides(head, tail, axis):
    count = lax.axis_size(axis)
    left = lax.ppermute(tail, axis, [(i, i + 1) for i in range(count - 1)])
    right = lax.ppermute(head, axis, [(i + 1, i) for i in range(count - 1)])
    return left, right


def exchanged(blocks, axis, unit):
    count = lax.axis_size(axis)
    return [
        lax.ppermute(block, axis, [(i, i ^ (turn * unit)) for i in range(count)])
        for turn, block in enumerate(blocks[1:], 1)
    ]


def swap(cells, axis):
    return lax.all_to_all(cells, axis, split_axis=0, concat_axis=0, tiled=True)


def spread_rows(rows, axis):
    count = lax.axis_size(axis)
    return swap(jnp.broadcast_to(rows[None], (count,) + rows.shape), axis)


def local(
    inputs, cotangent, conv_kernel, norm_gain, adapt_down, adapt_up, segment_lengths, segment_langs, lang_slot
):
    frames, width = inputs.shape[1:]
    units = adapt_down.shape[2]
    dp, ctx = lax.axis_size("dp"), lax.axis_size("ctx")
    rows = ctx * BLOCK
    own, cot = inputs[0], cotangent[0]
    gain = norm_gain.reshape(1, width)
    numbers = jnp.concatenate([segment_lengths.reshape(-1), segment_langs.reshape(-1), lang_slot])
    where = [("s", numbers)]

    left, right = from_sides(own[:EDGE], own[frames - EDGE :], "ctx")
    send, summed, inv = call(
        conv_and_norm,
        [((ctx, 2 * BLOCK, width), BF16), ((frames, width), F32), ((frames, LANES), F32)],
        where + [("v", left), ("v", own), ("v", right), ("v", cot), ("v", conv_kernel), ("v", gain)],
        [((frames + 2 * EDGE, width), F32), ((frames, width), BF16)],
    )
    got = swap(send, "ctx")
    back, pre_grad, act = call(
        keeper_back,
        [((rows, width), BF16), ((rows, 2 * units), BF16), ((rows, 2 * units), BF16)],
        [("v", got), ("v", adapt_down), ("v", adapt_up)],
    )
    grad_back = swap(back, "ctx")
    share = width // dp
    place = ("s", lax.axis_index("dp").astype(jnp.int32).reshape(1))
    kept, given = call(
        keeper_grads,
        [((dp // 2, 2 * share, 2 * units), F32), ((dp // 2, 2 * share, 2 * units), BF16)],
        [place, ("v", got), ("v", pre_grad), ("v", act)],
        [((width, 2 * units), F32), ((width, 2 * units), F32)],
    )
    (got,) = exchanged([kept, given], "dp", 1)
    grad_scale = 1.0 / math.sqrt(dp * ctx * frames)
    piece = (2 * share, 2 * units)
    chips = call(
        share_grads,
        [((2,) + piece, F32)] + [((2,) + piece, BF16)] * 3,
        [place, ("v", kept), ("v", got)],
    )
    got = exchanged(chips, "dp", 2)
    kept, given = call(
        pair_grads, [(piece, F32), (piece, BF16)], [place, ("v", chips[0])] + [("v", part) for part in got]
    )
    grad_back, kept, given = lax.optimization_barrier((grad_back, kept, given))
    total, edges, branch = call(
        sum_gradients,
        [((frames, width), F32), ((2, EDGE, width), F32), ((rows, width), BF16)],
        where
        + [("v", grad_back), ("v", cot), ("v", summed), ("v", inv), ("v", gain)]
        + [("v", left), ("v", own), ("v", right), ("v", act), ("v", adapt_up)],
        [((ctx, width), F32), ((frames + 2 * EDGE, width), F32), ((frames, width), F32)],
    )
    branch_back = swap(branch, "ctx")
    (got,) = exchanged([kept, given], "dp", 8)
    grad_down, grad_up = call(
        functools.partial(place_grads, grad_scale), [((2, share, units), F32)] * 2, [("v", kept), ("v", got)]
    )
    grad_left, grad_right = from_sides(edges[0], edges[1], "ctx")
    branch_back, grad_down, grad_up, grad_left, grad_right = lax.optimization_barrier(
        (branch_back, grad_down, grad_up, grad_left, grad_right)
    )
    (mine,) = call(sum_last_rows, [((8, width), F32)], [("v", branch_back)])
    (grad_input,) = call(
        input_gradient,
        [((frames, width), BF16)],
        [("v", grad_left), ("v", total), ("v", grad_right), ("v", conv_kernel)],
        [((frames + 2 * EDGE, width), F32)],
    )
    mine = spread_rows(mine[:1], "dp")
    mine, grad_input = lax.optimization_barrier((mine, grad_input))
    mine = jnp.sum(mine, axis=0) * grad_scale
    reduced = spread_rows(mine, "ctx").reshape(ctx, width)
    (output,) = call(add_branch, [((frames, width), BF16)], where + [("v", branch_back), ("v", summed)])
    return output[None], grad_input[None], reduced[:31], reduced[31], grad_down, jnp.transpose(grad_up, (0, 2, 1))


def solution(mesh):
    in_specs = (
        P("dp", "ctx", None),
        P("dp", "ctx", None),
        P(),
        P(),
        P("ctx", None, None),
        P("ctx", None, None),
        P("dp", "ctx", None),
        P("dp", "ctx", None),
        P(),
    )
    out_specs = (
        P("dp", "ctx", None),
        P("dp", "ctx", None),
        P(),
        P(),
        P("ctx", "dp", None),
        P("ctx", None, "dp"),
    )
    return jax.shard_map(local, mesh=mesh, in_specs=in_specs, out_specs=out_specs, check_vma=False)
```

```python
import functools
import math

import jax
import jax.numpy as jnp
from jax import lax
from jax.experimental import pallas as pl
from jax.experimental.pallas import tpu as pltpu
from jax.sharding import PartitionSpec as P

BLOCK = 16
SEGMENTS = 16
EDGE = 16
LANES = 128
VMEM = pl.BlockSpec(memory_space=pltpu.VMEM)
SMEM = pl.BlockSpec(memory_space=pltpu.SMEM)
PARAMS = pltpu.CompilerParams(vmem_limit_bytes=40 * 1024 * 1024)
F32 = jnp.float32
BF16 = jnp.bfloat16


HBM = pl.BlockSpec(memory_space=pltpu.HBM)
SPACES = {"s": SMEM, "v": VMEM, "h": HBM}


def call(body, outs, ins, scratch=(), copies=0):
    return pl.pallas_call(
        body,
        out_shape=tuple(jax.ShapeDtypeStruct(out[0], out[1]) for out in outs),
        in_specs=[SPACES[space] for space, _ in ins],
        out_specs=tuple(SPACES[(out + ("v",))[2]] for out in outs),
        scratch_shapes=[pltpu.VMEM(shape, kind) for shape, kind in scratch]
        + ([pltpu.SemaphoreType.DMA((copies,))] if copies else []),
        compiler_params=PARAMS,
    )(*[array for _, array in ins])


def started(pairs, sems, first=0):
    copies = [pltpu.make_async_copy(source, target, sems.at[first + at]) for at, (source, target) in enumerate(pairs)]
    for copy in copies:
        copy.start()
    return copies


def finish(copies):
    for copy in copies:
        copy.wait()


def segments(numbers):
    start = jnp.int32(0)
    found = []
    for seg in range(SEGMENTS):
        slot = numbers[2 * SEGMENTS + numbers[SEGMENTS + seg]]
        end = start + numbers[seg]
        found.append((start, end, slot // 2, slot % 2))
        start = end
    return found


def frame_slots(found, shape, dim):
    frame = lax.broadcasted_iota(jnp.int32, shape, dim)
    slot = jnp.zeros(shape, jnp.int32)
    for start, end, keeper, _ in found:
        slot = jnp.where((frame >= start) & (frame < end), keeper * BLOCK - start + frame, slot)
    return slot


def scatter_matrix(found, rows, frames):
    slot = frame_slots(found, (1, frames), 1)
    row = lax.broadcasted_iota(jnp.int32, (rows, frames), 0)
    return jnp.where(row == slot, 1.0, 0.0).astype(BF16)


def gather_matrix(found, rows, frames):
    slot = frame_slots(found, (frames, LANES), 0)
    lane = lax.broadcasted_iota(jnp.int32, (frames, LANES), 1)
    parts = [jnp.where(lane + at == slot, 1.0, 0.0) for at in range(0, rows, LANES)]
    return jnp.concatenate(parts, axis=1).astype(BF16)


def shifted(cells, by):
    return cells if by == 0 else pltpu.roll(cells, cells.shape[0] - by, 0)


def conv_and_norm(
    numbers, left_h, own_h, right_h, cot_h, taps_h, gain, send, summed_h, inv_h,
    cells, normed, left, own, right, cot, taps, summed, inv, sems,
):
    frames, width = own.shape
    loads = started([(cot_h, cot), (own_h, own), (left_h, left), (right_h, right), (taps_h, taps)], sems)
    rows = send.shape[0] * BLOCK
    blocks = (send.shape[0], BLOCK, width)
    found = segments(numbers)
    spread = scatter_matrix(found, rows, frames)
    row = lax.broadcasted_iota(jnp.int32, (rows, LANES), 0)
    mark = jnp.zeros((rows, LANES), F32)
    for _, _, keeper, which in found:
        mark = jnp.where(row == keeper * BLOCK + BLOCK - 1, which.astype(F32), mark)
    finish(loads[:1])
    moved = jnp.dot(spread, cot[...], preferred_element_type=F32)
    moved = jnp.concatenate([moved[:, :LANES] + mark, moved[:, LANES:]], axis=1)
    send[:, BLOCK:] = moved.astype(BF16).reshape(blocks)
    finish(loads[1:])
    cells[:EDGE] = left[...].astype(F32)
    cells[EDGE : EDGE + frames] = own[...].astype(F32)
    cells[EDGE + frames :] = right[...].astype(F32)
    half = frames // 2

    def column(at, squares):
        lanes = pl.ds(pl.multiple_of(at * LANES, LANES), LANES)
        sums = []
        for part in range(2):
            block = cells[part * half : part * half + half + 2 * EDGE, lanes]
            total = block[EDGE : EDGE + half]
            for low in range(8):
                moved = shifted(block, low)
                for high in range(0, 32, 8):
                    if high + low > 0:
                        tap = taps[high + low - 1 : high + low, lanes]
                        total = total + tap * moved[high : high + half]
            summed[part * half : part * half + half, lanes] = total
            sums.append(total * total)
        return squares + jnp.concatenate(sums, axis=0)

    squares = lax.fori_loop(0, width // LANES, column, jnp.zeros((frames, LANES), F32))
    scale = lax.rsqrt(jnp.sum(squares, axis=1, keepdims=True) * (1.0 / width) + 1e-06)
    inv[...] = jnp.broadcast_to(scale, inv.shape)
    stores = started([(summed, summed_h), (inv, inv_h)], sems, len(loads))
    normed[...] = (summed[...] * scale * gain[...]).astype(BF16)
    send[:, :BLOCK] = jnp.dot(spread, normed[...], preferred_element_type=F32).astype(BF16).reshape(blocks)
    finish(stores)


def received(got):
    shape = (got.shape[0] * BLOCK, got.shape[2])
    return got[:, :BLOCK].reshape(shape), got[:, BLOCK:].reshape(shape)


def keeper_back(got, down, up, back_h, pre_grad_h, act_h, back, pre_grad, act, sems):
    rows_in, cot_in = received(got)
    rows, width = rows_in.shape
    units = down.shape[2]
    marks = cot_in[:, :units].astype(F32).reshape(rows // BLOCK, BLOCK, units)
    marks = jnp.broadcast_to(marks[:, BLOCK - 1 :, :], marks.shape).reshape(rows, units)
    keep = jnp.concatenate([1.0 - marks, marks], axis=1)
    both_down = jnp.concatenate([down[0], down[1]], axis=1)
    both_up = up[...].reshape(2 * units, width)
    pre = jnp.dot(rows_in, both_down, preferred_element_type=F32)
    slope_of = lax.dot_general(cot_in, both_up, (((1,), (1,)), ((), ())), preferred_element_type=F32)
    sig = jax.nn.sigmoid(pre)
    act[...] = (keep * (pre * sig)).astype(BF16)
    grads = (keep * (slope_of * (sig * (1.0 + pre * (1.0 - sig))))).astype(BF16)
    pre_grad[...] = grads
    stores = started([(pre_grad, pre_grad_h), (act, act_h)], sems)
    back[...] = lax.dot_general(grads, both_down, (((1,), (1,)), ((), ())), preferred_element_type=F32).astype(BF16)
    finish(started([(back, back_h)], sems, len(stores)) + stores)


def sum_last_rows(back, out):
    row = lax.broadcasted_iota(jnp.int32, (out.shape[0], back.shape[0]), 1)
    last = jnp.where(row % BLOCK == BLOCK - 1, 1.0, 0.0).astype(BF16)
    out[...] = jnp.dot(last, back[...], preferred_element_type=F32)


def keeper_grads(place, got, pre_grad, act, kept, given, down, up):
    parts, twice, _ = kept.shape
    part = twice // 2
    core = place[0] % 2
    rows_in, cot_in = received(got)
    down[...] = lax.dot_general(rows_in, pre_grad[...], (((0,), (0,)), ((), ())), preferred_element_type=F32)
    up[...] = lax.dot_general(cot_in, act[...], (((0,), (0,)), ((), ())), preferred_element_type=F32)
    for at in range(parts):
        near = pl.ds(pl.multiple_of((2 * at + core) * part, part), part)
        far = pl.ds(pl.multiple_of((2 * at + 1 - core) * part, part), part)
        kept[at, :part] = down[near]
        kept[at, part:] = up[near]
        given[at, :part] = down[far].astype(BF16)
        given[at, part:] = up[far].astype(BF16)


def share_grads(place, kept, got, own, *given):
    chip = place[0] // 2
    for turn, out in enumerate((own,) + given):
        for high in range(out.shape[0]):
            at = 4 * high + ((chip % 4) ^ turn)
            out[high] = (kept[at] + got[at].astype(F32)).astype(out.dtype)


def pair_grads(place, own, first, second, third, kept, given):
    high = place[0] // 8
    for at, out in ((high, kept), (1 - high, given)):
        total = own[at] + first[at].astype(F32) + second[at].astype(F32) + third[at].astype(F32)
        out[...] = total.astype(out.dtype)


def sum_gradients(
    numbers, gain, back_h, summed_h, inv_h, cot_h, own_h, left_h, right_h, act_h, up_h, total_h, edges_h, branch_h,
    sums, cells, frames_grad, back, summed, inv, cot, own, left, right, act, up, total, branch, sems,
):
    frames, width = cot.shape
    loads = started(
        [(back_h, back), (summed_h, summed), (inv_h, inv), (cot_h, cot), (own_h, own)]
        + [(left_h, left), (right_h, right), (act_h, act), (up_h, up)],
        sems,
    )
    gather = gather_matrix(segments(numbers), back.shape[0], frames)
    finish(loads[:1])
    frames_grad[...] = jnp.dot(gather, back[...], preferred_element_type=F32)
    finish(loads[1:7])
    cells[:EDGE] = left[...].astype(F32)
    cells[EDGE : EDGE + frames] = own[...].astype(F32)
    cells[EDGE + frames :] = right[...].astype(F32)
    scale = inv[:, :1]
    inner = jnp.sum(gain[...] * frames_grad[...] * summed[...], axis=1, keepdims=True) * (1.0 / width)
    pull = scale * scale * scale * inner
    half = frames // 2

    def column(at, carry):
        lanes = pl.ds(pl.multiple_of(at * LANES, LANES), LANES)
        for part in range(2):
            span = slice(part * half, part * half + half)
            grad = frames_grad[span, lanes]
            base = summed[span, lanes]
            inverse = inv[span, :]
            gain_sum = jnp.sum(grad * base * inverse, axis=0, keepdims=True)
            whole = cot[span, lanes].astype(F32) + inverse * (gain[:, lanes] * grad) - base * pull[span]
            total[span, lanes] = whole
            block = cells[part * half : part * half + half + 2 * EDGE, lanes]
            found = [None] * 31
            for low in range(8):
                moved = shifted(block, low)
                for high in range(0, 32, 8):
                    if high + low > 0:
                        product = whole * moved[high : high + half]
                        found[high + low - 1] = jnp.sum(product, axis=0, keepdims=True)
            rows = jnp.concatenate(found + [gain_sum], axis=0)
            if part == 0:
                first = rows
            else:
                sums[:, lanes] = first + rows
        return carry

    lax.fori_loop(0, width // LANES, column, 0)
    ends = [(total.at[pl.ds(0, EDGE)], edges_h.at[0]), (total.at[pl.ds(frames - EDGE, EDGE)], edges_h.at[1])]
    stores = started(ends + [(total, total_h)], sems, len(loads))
    finish(loads[7:])
    both_up = up[...].reshape(act.shape[1], width)
    row = lax.broadcasted_iota(jnp.int32, (branch.shape[0], sums.shape[0]), 0)
    block = lax.broadcasted_iota(jnp.int32, (branch.shape[0], sums.shape[0]), 1)
    last = jnp.where(row == block * BLOCK + BLOCK - 1, 1.0, 0.0).astype(BF16)
    outputs = jnp.dot(act[...], both_up, preferred_element_type=F32)
    outputs = outputs + jnp.dot(last, sums[...].astype(BF16), preferred_element_type=F32)
    branch[...] = outputs.astype(BF16)
    finish(started([(branch, branch_h)], sems, len(loads) + len(stores)) + stores)


def input_gradient(left, own, right, taps, out, cells):
    frames, width = own.shape
    cells[:EDGE] = left[...]
    cells[EDGE : EDGE + frames] = own[...]
    cells[EDGE + frames :] = right[...]
    half = frames // 2

    def column(at, carry):
        lanes = pl.ds(pl.multiple_of(at * LANES, LANES), LANES)
        for part in range(2):
            block = cells[part * half : part * half + half + 2 * EDGE, lanes]
            total = block[EDGE : EDGE + half]
            for low in range(8):
                moved = shifted(block, low)
                for high in range(0, 32, 8):
                    if high + low > 0:
                        tap = taps[31 - high - low : 32 - high - low, lanes]
                        total = total + tap * moved[high : high + half]
            out[part * half : part * half + half, lanes] = total.astype(BF16)
        return carry

    lax.fori_loop(0, width // LANES, column, 0)


def add_branch(numbers, back, summed, out):
    gather = gather_matrix(segments(numbers), back.shape[0], summed.shape[0])
    out[...] = (summed[...] + jnp.dot(gather, back[...], preferred_element_type=F32)).astype(BF16)


def place_grads(scale, kept, got, down, up):
    share, units = down.shape[1:]
    total = (kept[...] + got[...].astype(F32)) * scale
    for which in range(2):
        lanes = slice(which * units, which * units + units)
        down[which] = total[:share, lanes]
        up[which] = total[share:, lanes]


def from_sides(head, tail, axis):
    count = lax.axis_size(axis)
    left = lax.ppermute(tail, axis, [(i, i + 1) for i in range(count - 1)])
    right = lax.ppermute(head, axis, [(i + 1, i) for i in range(count - 1)])
    return left, right


def exchanged(blocks, axis, unit):
    count = lax.axis_size(axis)
    return [
        lax.ppermute(block, axis, [(i, i ^ (turn * unit)) for i in range(count)])
        for turn, block in enumerate(blocks[1:], 1)
    ]


def swap(cells, axis):
    return lax.all_to_all(cells, axis, split_axis=0, concat_axis=0, tiled=True)


def spread_rows(rows, axis):
    count = lax.axis_size(axis)
    return swap(jnp.broadcast_to(rows[None], (count,) + rows.shape), axis)


def local(
    inputs, cotangent, conv_kernel, norm_gain, adapt_down, adapt_up, segment_lengths, segment_langs, lang_slot
):
    frames, width = inputs.shape[1:]
    units = adapt_down.shape[2]
    dp, ctx = lax.axis_size("dp"), lax.axis_size("ctx")
    rows = ctx * BLOCK
    own, cot = inputs[0], cotangent[0]
    gain = norm_gain.reshape(1, width)
    numbers = jnp.concatenate([segment_lengths.reshape(-1), segment_langs.reshape(-1), lang_slot])
    where = [("s", numbers)]

    left, right = from_sides(own[:EDGE], own[frames - EDGE :], "ctx")
    send, summed, inv = call(
        conv_and_norm,
        [((ctx, 2 * BLOCK, width), BF16), ((frames, width), F32, "h"), ((frames, LANES), F32, "h")],
        where + [("h", left), ("h", own), ("h", right), ("h", cot), ("h", conv_kernel), ("v", gain)],
        [((frames + 2 * EDGE, width), F32), ((frames, width), BF16)]
        + [((EDGE, width), BF16), ((frames, width), BF16), ((EDGE, width), BF16), ((frames, width), BF16)]
        + [(conv_kernel.shape, F32), ((frames, width), F32), ((frames, LANES), F32)],
        copies=7,
    )
    got = swap(send, "ctx")
    back, pre_grad, act = call(
        keeper_back,
        [((rows, width), BF16, "h"), ((rows, 2 * units), BF16, "h"), ((rows, 2 * units), BF16, "h")],
        [("v", got), ("v", adapt_down), ("v", adapt_up)],
        [((rows, width), BF16), ((rows, 2 * units), BF16), ((rows, 2 * units), BF16)],
        copies=3,
    )
    grad_back = swap(back, "ctx")
    share = width // dp
    place = ("s", lax.axis_index("dp").astype(jnp.int32).reshape(1))
    kept, given = call(
        keeper_grads,
        [((dp // 2, 2 * share, 2 * units), F32), ((dp // 2, 2 * share, 2 * units), BF16)],
        [place, ("v", got), ("v", pre_grad), ("v", act)],
        [((width, 2 * units), F32), ((width, 2 * units), F32)],
    )
    (got,) = exchanged([kept, given], "dp", 1)
    grad_scale = 1.0 / math.sqrt(dp * ctx * frames)
    piece = (2 * share, 2 * units)
    chips = call(
        share_grads,
        [((2,) + piece, F32)] + [((2,) + piece, BF16)] * 3,
        [place, ("v", kept), ("v", got)],
    )
    got = exchanged(chips, "dp", 2)
    kept, given = call(
        pair_grads, [(piece, F32), (piece, BF16)], [place, ("v", chips[0])] + [("v", part) for part in got]
    )
    grad_back, kept, given = lax.optimization_barrier((grad_back, kept, given))
    total, edges, branch = call(
        sum_gradients,
        [((frames, width), F32, "h"), ((2, EDGE, width), F32, "h"), ((rows, width), BF16, "h")],
        where
        + [("v", gain), ("h", grad_back), ("h", summed), ("h", inv), ("h", cot), ("h", own)]
        + [("h", left), ("h", right), ("h", act), ("h", adapt_up)],
        [((ctx, width), F32), ((frames + 2 * EDGE, width), F32), ((frames, width), F32), ((rows, width), BF16)]
        + [((frames, width), F32), ((frames, LANES), F32), ((frames, width), BF16), ((frames, width), BF16)]
        + [((EDGE, width), BF16), ((EDGE, width), BF16), ((rows, 2 * units), BF16), (adapt_up.shape, BF16)]
        + [((frames, width), F32), ((rows, width), BF16)],
        copies=13,
    )
    branch_back = swap(branch, "ctx")
    (got,) = exchanged([kept, given], "dp", 8)
    grad_down, grad_up = call(
        functools.partial(place_grads, grad_scale), [((2, share, units), F32)] * 2, [("v", kept), ("v", got)]
    )
    grad_left, grad_right = from_sides(edges[0], edges[1], "ctx")
    branch_back, grad_down, grad_up, grad_left, grad_right = lax.optimization_barrier(
        (branch_back, grad_down, grad_up, grad_left, grad_right)
    )
    (mine,) = call(sum_last_rows, [((8, width), F32)], [("v", branch_back)])
    (grad_input,) = call(
        input_gradient,
        [((frames, width), BF16)],
        [("v", grad_left), ("v", total), ("v", grad_right), ("v", conv_kernel)],
        [((frames + 2 * EDGE, width), F32)],
    )
    mine = spread_rows(mine[:1], "dp")
    mine, grad_input = lax.optimization_barrier((mine, grad_input))
    mine = jnp.sum(mine, axis=0) * grad_scale
    reduced = spread_rows(mine, "ctx").reshape(ctx, width)
    (output,) = call(add_branch, [((frames, width), BF16)], where + [("v", branch_back), ("v", summed)])
    return output[None], grad_input[None], reduced[:31], reduced[31], grad_down, jnp.transpose(grad_up, (0, 2, 1))


def solution(mesh):
    in_specs = (
        P("dp", "ctx", None),
        P("dp", "ctx", None),
        P(),
        P(),
        P("ctx", None, None),
        P("ctx", None, None),
        P("dp", "ctx", None),
        P("dp", "ctx", None),
        P(),
    )
    out_specs = (
        P("dp", "ctx", None),
        P("dp", "ctx", None),
        P(),
        P(),
        P("ctx", "dp", None),
        P("ctx", None, "dp"),
    )
    return jax.shard_map(local, mesh=mesh, in_specs=in_specs, out_specs=out_specs, check_vma=False)
```

```python
import functools
import math

import jax
import jax.numpy as jnp
from jax import lax
from jax.experimental import pallas as pl
from jax.experimental.pallas import tpu as pltpu
from jax.sharding import PartitionSpec as P

BLOCK = 16
HALF = BLOCK // 2
SEGMENTS = 16
EDGE = 16
LANES = 128
VMEM = pl.BlockSpec(memory_space=pltpu.VMEM)
SMEM = pl.BlockSpec(memory_space=pltpu.SMEM)
PARAMS = pltpu.CompilerParams(vmem_limit_bytes=40 * 1024 * 1024)
F32 = jnp.float32
BF16 = jnp.bfloat16


def call(body, outs, ins, scratch=()):
    return pl.pallas_call(
        body,
        out_shape=tuple(jax.ShapeDtypeStruct(shape, kind) for shape, kind in outs),
        in_specs=[SMEM if space == "s" else VMEM for space, _ in ins],
        out_specs=tuple(VMEM for _ in outs),
        scratch_shapes=[pltpu.VMEM(shape, kind) for shape, kind in scratch],
        compiler_params=PARAMS,
    )(*[array for _, array in ins])


def segments(numbers):
    start = jnp.int32(0)
    found = []
    for seg in range(SEGMENTS):
        slot = numbers[2 * SEGMENTS + numbers[SEGMENTS + seg]]
        end = start + numbers[seg]
        found.append((start, end, slot // 2, slot % 2))
        start = end
    return found


def frame_slots(found, shape, dim):
    frame = lax.broadcasted_iota(jnp.int32, shape, dim)
    slot = jnp.zeros(shape, jnp.int32)
    for start, end, keeper, _ in found:
        slot = jnp.where((frame >= start) & (frame < end), keeper * BLOCK - start + frame, slot)
    return slot


def scatter_matrix(found, rows, frames):
    slot = frame_slots(found, (1, frames), 1)
    row = lax.broadcasted_iota(jnp.int32, (rows, frames), 0)
    return jnp.where(row == slot, 1.0, 0.0).astype(BF16)


def gather_matrix(found, rows, frames):
    slot = frame_slots(found, (frames, LANES), 0)
    lane = lax.broadcasted_iota(jnp.int32, (frames, LANES), 1)
    parts = [jnp.where(lane + at == slot, 1.0, 0.0) for at in range(0, rows, LANES)]
    return jnp.concatenate(parts, axis=1).astype(BF16)


def shifted(cells, by):
    return cells if by == 0 else pltpu.roll(cells, cells.shape[0] - by, 0)


def conv_and_norm(numbers, left, own, right, cot, taps, gain, send, summed, cells, normed):
    frames, width = own.shape
    rows = send.shape[0] * BLOCK
    blocks = (send.shape[0], BLOCK, width)
    found = segments(numbers)
    spread = scatter_matrix(found, rows, frames)
    row = lax.broadcasted_iota(jnp.int32, (rows, LANES), 0)
    mark = jnp.zeros((rows, LANES), F32)
    for _, _, keeper, which in found:
        mark = jnp.where(row == keeper * BLOCK + BLOCK - 1, which.astype(F32), mark)
    moved = jnp.dot(spread, cot[...], preferred_element_type=F32)
    moved = jnp.concatenate([moved[:, :LANES] + mark, moved[:, LANES:]], axis=1)
    send[:, BLOCK:] = moved.astype(BF16).reshape(blocks)
    cells[:EDGE] = left[...].astype(F32)
    cells[EDGE : EDGE + frames] = own[...].astype(F32)
    cells[EDGE + frames :] = right[...].astype(F32)
    half = frames // 2

    def column(at, squares):
        lanes = pl.ds(pl.multiple_of(at * LANES, LANES), LANES)
        sums = []
        for part in range(2):
            block = cells[part * half : part * half + half + 2 * EDGE, lanes]
            total = block[EDGE : EDGE + half]
            for low in range(8):
                moved = shifted(block, low)
                for high in range(0, 32, 8):
                    if high + low > 0:
                        tap = taps[high + low - 1 : high + low, lanes]
                        total = total + tap * moved[high : high + half]
            summed[part * half : part * half + half, lanes] = total
            sums.append(total * total)
        return squares + jnp.concatenate(sums, axis=0)

    squares = lax.fori_loop(0, width // LANES, column, jnp.zeros((frames, LANES), F32))
    scale = lax.rsqrt(jnp.sum(squares, axis=1, keepdims=True) * (1.0 / width) + 1e-06)
    normed[...] = (summed[...] * scale * gain[...]).astype(BF16)
    send[:, :BLOCK] = jnp.dot(spread, normed[...], preferred_element_type=F32).astype(BF16).reshape(blocks)


def received(got):
    shape = (got.shape[0] * BLOCK, got.shape[2])
    return got[:, :BLOCK].reshape(shape), got[:, BLOCK:].reshape(shape)


def keeper_values(got, down, up):
    rows_in, cot_in = received(got)
    rows, width = rows_in.shape
    units = down.shape[2]
    marks = cot_in[:, :units].astype(F32).reshape(rows // BLOCK, BLOCK, units)
    marks = jnp.broadcast_to(marks[:, BLOCK - 1 :, :], marks.shape).reshape(rows, units)
    keep = jnp.concatenate([1.0 - marks, marks], axis=1)
    both_down = jnp.concatenate([down[0], down[1]], axis=1)
    both_up = up[...].reshape(2 * units, width)
    pre = jnp.dot(rows_in, both_down, preferred_element_type=F32)
    slope_of = lax.dot_general(cot_in, both_up, (((1,), (1,)), ((), ())), preferred_element_type=F32)
    sig = jax.nn.sigmoid(pre)
    act = (keep * (pre * sig)).astype(BF16)
    grads = (keep * (slope_of * (sig * (1.0 + pre * (1.0 - sig))))).astype(BF16)
    return rows_in, cot_in, both_down, grads, act


def keeper_back(got, down, up, back):
    _, _, both_down, grads, _ = keeper_values(got, down, up)
    back[...] = lax.dot_general(grads, both_down, (((1,), (1,)), ((), ())), preferred_element_type=F32).astype(BF16)


def sum_last_rows(back, out):
    row = lax.broadcasted_iota(jnp.int32, (out.shape[0], back.shape[0]), 1)
    last = jnp.where(row % HALF == HALF - 1, 1.0, 0.0).astype(BF16)
    out[...] = jnp.dot(last, back[...], preferred_element_type=F32)


def keeper_grads(place, got, down_w, up_w, kept, given, act, down, up):
    parts, twice, _ = kept.shape
    part = twice // 2
    core = place[0] % 2
    rows_in, cot_in, _, grads, acts = keeper_values(got, down_w, up_w)
    act[...] = acts
    down[...] = lax.dot_general(rows_in, grads, (((0,), (0,)), ((), ())), preferred_element_type=F32)
    up[...] = lax.dot_general(cot_in, acts, (((0,), (0,)), ((), ())), preferred_element_type=F32)
    for at in range(parts):
        near = pl.ds(pl.multiple_of((2 * at + core) * part, part), part)
        far = pl.ds(pl.multiple_of((2 * at + 1 - core) * part, part), part)
        kept[at, :part] = down[near]
        kept[at, part:] = up[near]
        given[at, :part] = down[far].astype(BF16)
        given[at, part:] = up[far].astype(BF16)


def share_grads(place, kept, got, own, *given):
    chip = place[0] // 2
    for turn, out in enumerate((own,) + given):
        for high in range(out.shape[0]):
            at = 4 * high + ((chip % 4) ^ turn)
            out[high] = (kept[at] + got[at].astype(F32)).astype(out.dtype)


def pair_grads(place, own, first, second, third, kept, given):
    high = place[0] // 8
    for at, out in ((high, kept), (1 - high, given)):
        total = own[at] + first[at].astype(F32) + second[at].astype(F32) + third[at].astype(F32)
        out[...] = total.astype(out.dtype)


def sum_gradients(
    numbers, back, cot, summed, gain, left, own, right, act, up, total, edges, low, high, sums, cells, frames_grad, inv
):
    frames, width = cot.shape
    gather = gather_matrix(segments(numbers), back.shape[0], frames)
    cells[:EDGE] = left[...].astype(F32)
    cells[EDGE : EDGE + frames] = own[...].astype(F32)
    cells[EDGE + frames :] = right[...].astype(F32)
    frames_grad[...] = jnp.dot(gather, back[...], preferred_element_type=F32)
    scale = lax.rsqrt(jnp.sum(summed[...] * summed[...], axis=1, keepdims=True) * (1.0 / width) + 1e-06)
    inv[...] = jnp.broadcast_to(scale, inv.shape)
    inner = jnp.sum(gain[...] * frames_grad[...] * summed[...], axis=1, keepdims=True) * (1.0 / width)
    pull = scale * scale * scale * inner
    half = frames // 2

    def column(at, carry):
        lanes = pl.ds(pl.multiple_of(at * LANES, LANES), LANES)
        for part in range(2):
            span = slice(part * half, part * half + half)
            grad = frames_grad[span, lanes]
            base = summed[span, lanes]
            inverse = inv[span, :]
            gain_sum = jnp.sum(grad * base * inverse, axis=0, keepdims=True)
            whole = cot[span, lanes].astype(F32) + inverse * (gain[:, lanes] * grad) - base * pull[span]
            total[span, lanes] = whole
            block = cells[part * half : part * half + half + 2 * EDGE, lanes]
            found = [None] * 31
            for low in range(8):
                moved = shifted(block, low)
                for high in range(0, 32, 8):
                    if high + low > 0:
                        product = whole * moved[high : high + half]
                        found[high + low - 1] = jnp.sum(product, axis=0, keepdims=True)
            rows = jnp.concatenate(found + [gain_sum], axis=0)
            if part == 0:
                first = rows
            else:
                sums[:, lanes] = first + rows
        return carry

    lax.fori_loop(0, width // LANES, column, 0)
    edges[0] = total[:EDGE]
    edges[1] = total[frames - EDGE :]
    both_up = up[...].reshape(act.shape[1], width)
    count, blocks = act.shape[0], sums.shape[0]
    row = lax.broadcasted_iota(jnp.int32, (count, blocks), 0)
    block = lax.broadcasted_iota(jnp.int32, (count, blocks), 1)
    last = jnp.where(row == block * BLOCK + BLOCK - 1, 1.0, 0.0).astype(BF16)
    branch = jnp.dot(act[...], both_up, preferred_element_type=F32)
    branch = branch + jnp.dot(last, sums[...].astype(BF16), preferred_element_type=F32)
    branch = branch.reshape(blocks, BLOCK, width)
    low[...] = branch[:, :HALF].reshape(low.shape).astype(BF16)
    high[...] = branch[:, HALF:].reshape(high.shape).astype(BF16)


def input_gradient(left, own, right, taps, out, cells):
    frames, width = own.shape
    cells[:EDGE] = left[...]
    cells[EDGE : EDGE + frames] = own[...]
    cells[EDGE + frames :] = right[...]
    half = frames // 2

    def column(at, carry):
        lanes = pl.ds(pl.multiple_of(at * LANES, LANES), LANES)
        for part in range(2):
            block = cells[part * half : part * half + half + 2 * EDGE, lanes]
            total = block[EDGE : EDGE + half]
            for low in range(8):
                moved = shifted(block, low)
                for high in range(0, 32, 8):
                    if high + low > 0:
                        tap = taps[31 - high - low : 32 - high - low, lanes]
                        total = total + tap * moved[high : high + half]
            out[part * half : part * half + half, lanes] = total.astype(BF16)
        return carry

    lax.fori_loop(0, width // LANES, column, 0)


def add_branch(numbers, low, high, summed, out):
    frames = summed.shape[0]
    slot = frame_slots(segments(numbers), (frames, LANES), 0)
    lane = lax.broadcasted_iota(jnp.int32, (frames, LANES), 1)
    within = slot % BLOCK
    place = (slot // BLOCK) * HALF + within % HALF
    total = summed[...]
    for part, first in ((low, True), (high, False)):
        here = (within < HALF) if first else (within >= HALF)
        hits = [jnp.where(here & (lane + at == place), 1.0, 0.0) for at in range(0, part.shape[0], LANES)]
        total = total + jnp.dot(jnp.concatenate(hits, axis=1).astype(BF16), part[...], preferred_element_type=F32)
    out[...] = total.astype(BF16)


def place_grads(scale, kept, got, down, up):
    share, units = down.shape[1:]
    total = (kept[...] + got[...].astype(F32)) * scale
    for which in range(2):
        lanes = slice(which * units, which * units + units)
        down[which] = total[:share, lanes]
        up[which] = total[share:, lanes]


def from_sides(head, tail, axis):
    count = lax.axis_size(axis)
    left = lax.ppermute(tail, axis, [(i, i + 1) for i in range(count - 1)])
    right = lax.ppermute(head, axis, [(i + 1, i) for i in range(count - 1)])
    return left, right


def exchanged(blocks, axis, unit):
    count = lax.axis_size(axis)
    return [
        lax.ppermute(block, axis, [(i, i ^ (turn * unit)) for i in range(count)])
        for turn, block in enumerate(blocks[1:], 1)
    ]


def swap(cells, axis):
    return lax.all_to_all(cells, axis, split_axis=0, concat_axis=0, tiled=True)


def spread_rows(rows, axis):
    count = lax.axis_size(axis)
    return swap(jnp.broadcast_to(rows[None], (count,) + rows.shape), axis)


def local(
    inputs, cotangent, conv_kernel, norm_gain, adapt_down, adapt_up, segment_lengths, segment_langs, lang_slot
):
    frames, width = inputs.shape[1:]
    units = adapt_down.shape[2]
    dp, ctx = lax.axis_size("dp"), lax.axis_size("ctx")
    rows = ctx * BLOCK
    own, cot = inputs[0], cotangent[0]
    gain = norm_gain.reshape(1, width)
    numbers = jnp.concatenate([segment_lengths.reshape(-1), segment_langs.reshape(-1), lang_slot])
    where = [("s", numbers)]

    left, right = from_sides(own[:EDGE], own[frames - EDGE :], "ctx")
    send, summed = call(
        conv_and_norm,
        [((ctx, 2 * BLOCK, width), BF16), ((frames, width), F32)],
        where + [("v", left), ("v", own), ("v", right), ("v", cot), ("v", conv_kernel), ("v", gain)],
        [((frames + 2 * EDGE, width), F32), ((frames, width), BF16)],
    )
    got = swap(send, "ctx")
    (back,) = call(
        keeper_back, [((rows, width), BF16)], [("v", got), ("v", adapt_down), ("v", adapt_up)]
    )
    grad_back = swap(back, "ctx")
    share = width // dp
    place = ("s", lax.axis_index("dp").astype(jnp.int32).reshape(1))
    kept, given, act = call(
        keeper_grads,
        [((dp // 2, 2 * share, 2 * units), F32), ((dp // 2, 2 * share, 2 * units), BF16), ((rows, 2 * units), BF16)],
        [place, ("v", got), ("v", adapt_down), ("v", adapt_up)],
        [((width, 2 * units), F32), ((width, 2 * units), F32)],
    )
    (got,) = exchanged([kept, given], "dp", 1)
    grad_scale = 1.0 / math.sqrt(dp * ctx * frames)
    piece = (2 * share, 2 * units)
    chips = call(
        share_grads,
        [((2,) + piece, F32)] + [((2,) + piece, BF16)] * 3,
        [place, ("v", kept), ("v", got)],
    )
    got = exchanged(chips, "dp", 2)
    kept, given = call(
        pair_grads, [(piece, F32), (piece, BF16)], [place, ("v", chips[0])] + [("v", part) for part in got]
    )
    grad_back, kept, given = lax.optimization_barrier((grad_back, kept, given))
    total, edges, low, high = call(
        sum_gradients,
        [((frames, width), F32), ((2, EDGE, width), F32), ((rows // 2, width), BF16), ((rows // 2, width), BF16)],
        where
        + [("v", grad_back), ("v", cot), ("v", summed), ("v", gain)]
        + [("v", left), ("v", own), ("v", right), ("v", act), ("v", adapt_up)],
        [((ctx, width), F32), ((frames + 2 * EDGE, width), F32), ((frames, width), F32), ((frames, LANES), F32)],
    )
    high_back = swap(high, "ctx")
    (got,) = exchanged([kept, given], "dp", 8)
    grad_down, grad_up = call(
        functools.partial(place_grads, grad_scale), [((2, share, units), F32)] * 2, [("v", kept), ("v", got)]
    )
    grad_left, grad_right = from_sides(edges[0], edges[1], "ctx")
    high_back, low, grad_down, grad_up, grad_left, grad_right = lax.optimization_barrier(
        (high_back, low, grad_down, grad_up, grad_left, grad_right)
    )
    low_back = swap(low, "ctx")
    (mine,) = call(sum_last_rows, [((8, width), F32)], [("v", high_back)])
    mine = lax.all_gather(mine[:1], "dp", axis=0, tiled=True)
    (grad_input,) = call(
        input_gradient,
        [((frames, width), BF16)],
        [("v", grad_left), ("v", total), ("v", grad_right), ("v", conv_kernel)],
        [((frames + 2 * EDGE, width), F32)],
    )
    mine, low_back, grad_input = lax.optimization_barrier((mine, low_back, grad_input))
    mine = jnp.sum(mine, axis=0, keepdims=True) * grad_scale
    reduced = spread_rows(mine, "ctx").reshape(ctx, width)
    (output,) = call(
        add_branch,
        [((frames, width), BF16)],
        where + [("v", low_back), ("v", high_back), ("v", summed)],
    )
    return output[None], grad_input[None], reduced[:31], reduced[31], grad_down, jnp.transpose(grad_up, (0, 2, 1))


def solution(mesh):
    in_specs = (
        P("dp", "ctx", None),
        P("dp", "ctx", None),
        P(),
        P(),
        P("ctx", None, None),
        P("ctx", None, None),
        P("dp", "ctx", None),
        P("dp", "ctx", None),
        P(),
    )
    out_specs = (
        P("dp", "ctx", None),
        P("dp", "ctx", None),
        P(),
        P(),
        P("ctx", "dp", None),
        P("ctx", None, "dp"),
    )
    return jax.shard_map(local, mesh=mesh, in_specs=in_specs, out_specs=out_specs, check_vma=False)
```

```python
import functools
import math

import jax
import jax.numpy as jnp
from jax import lax
from jax.experimental import pallas as pl
from jax.experimental.pallas import tpu as pltpu
from jax.sharding import PartitionSpec as P

BLOCK = 16
HALF = BLOCK // 2
SEGMENTS = 16
EDGE = 16
LANES = 128
VMEM = pl.BlockSpec(memory_space=pltpu.VMEM)
SMEM = pl.BlockSpec(memory_space=pltpu.SMEM)
PARAMS = pltpu.CompilerParams(vmem_limit_bytes=40 * 1024 * 1024)
F32 = jnp.float32
BF16 = jnp.bfloat16


def call(body, outs, ins, scratch=()):
    return pl.pallas_call(
        body,
        out_shape=tuple(jax.ShapeDtypeStruct(shape, kind) for shape, kind in outs),
        in_specs=[SMEM if space == "s" else VMEM for space, _ in ins],
        out_specs=tuple(VMEM for _ in outs),
        scratch_shapes=[pltpu.VMEM(shape, kind) for shape, kind in scratch],
        compiler_params=PARAMS,
    )(*[array for _, array in ins])


def segments(numbers):
    start = jnp.int32(0)
    found = []
    for seg in range(SEGMENTS):
        slot = numbers[2 * SEGMENTS + numbers[SEGMENTS + seg]]
        end = start + numbers[seg]
        found.append((start, end, slot // 2, slot % 2))
        start = end
    return found


def frame_slots(found, shape, dim):
    frame = lax.broadcasted_iota(jnp.int32, shape, dim)
    slot = jnp.zeros(shape, jnp.int32)
    for start, end, keeper, _ in found:
        slot = jnp.where((frame >= start) & (frame < end), keeper * BLOCK - start + frame, slot)
    return slot


def scatter_matrix(found, rows, frames):
    slot = frame_slots(found, (1, frames), 1)
    row = lax.broadcasted_iota(jnp.int32, (rows, frames), 0)
    return jnp.where(row == slot, 1.0, 0.0).astype(BF16)


def gather_matrix(found, rows, frames):
    slot = frame_slots(found, (frames, LANES), 0)
    lane = lax.broadcasted_iota(jnp.int32, (frames, LANES), 1)
    parts = [jnp.where(lane + at == slot, 1.0, 0.0) for at in range(0, rows, LANES)]
    return jnp.concatenate(parts, axis=1).astype(BF16)


def shifted(cells, by):
    return cells if by == 0 else pltpu.roll(cells, cells.shape[0] - by, 0)


def conv_and_norm(numbers, left, own, right, cot, taps, gain, send, summed, cells, normed):
    frames, width = own.shape
    rows = send.shape[0] * BLOCK
    blocks = (send.shape[0], BLOCK, width)
    found = segments(numbers)
    spread = scatter_matrix(found, rows, frames)
    row = lax.broadcasted_iota(jnp.int32, (rows, LANES), 0)
    mark = jnp.zeros((rows, LANES), F32)
    for _, _, keeper, which in found:
        mark = jnp.where(row == keeper * BLOCK + BLOCK - 1, which.astype(F32), mark)
    moved = jnp.dot(spread, cot[...], preferred_element_type=F32)
    moved = jnp.concatenate([moved[:, :LANES] + mark, moved[:, LANES:]], axis=1)
    send[:, BLOCK:] = moved.astype(BF16).reshape(blocks)
    cells[:EDGE] = left[...].astype(F32)
    cells[EDGE : EDGE + frames] = own[...].astype(F32)
    cells[EDGE + frames :] = right[...].astype(F32)
    half = frames // 2

    def column(at, squares):
        lanes = pl.ds(pl.multiple_of(at * LANES, LANES), LANES)
        sums = []
        for part in range(2):
            block = cells[part * half : part * half + half + 2 * EDGE, lanes]
            total = block[EDGE : EDGE + half]
            for low in range(8):
                moved = shifted(block, low)
                for high in range(0, 32, 8):
                    if high + low > 0:
                        tap = taps[high + low - 1 : high + low, lanes]
                        total = total + tap * moved[high : high + half]
            summed[part * half : part * half + half, lanes] = total
            sums.append(total * total)
        return squares + jnp.concatenate(sums, axis=0)

    squares = lax.fori_loop(0, width // LANES, column, jnp.zeros((frames, LANES), F32))
    scale = lax.rsqrt(jnp.sum(squares, axis=1, keepdims=True) * (1.0 / width) + 1e-06)
    normed[...] = (summed[...] * scale * gain[...]).astype(BF16)
    send[:, :BLOCK] = jnp.dot(spread, normed[...], preferred_element_type=F32).astype(BF16).reshape(blocks)


def received(got):
    shape = (got.shape[0] * BLOCK, got.shape[2])
    return got[:, :BLOCK].reshape(shape), got[:, BLOCK:].reshape(shape)


def keeper_values(got, down, up):
    rows_in, cot_in = received(got)
    rows, width = rows_in.shape
    units = down.shape[2]
    marks = cot_in[:, :units].astype(F32).reshape(rows // BLOCK, BLOCK, units)
    marks = jnp.broadcast_to(marks[:, BLOCK - 1 :, :], marks.shape).reshape(rows, units)
    keep = jnp.concatenate([1.0 - marks, marks], axis=1)
    both_down = jnp.concatenate([down[0], down[1]], axis=1)
    both_up = up[...].reshape(2 * units, width)
    pre = jnp.dot(rows_in, both_down, preferred_element_type=F32)
    slope_of = lax.dot_general(cot_in, both_up, (((1,), (1,)), ((), ())), preferred_element_type=F32)
    sig = jax.nn.sigmoid(pre)
    act = (keep * (pre * sig)).astype(BF16)
    grads = (keep * (slope_of * (sig * (1.0 + pre * (1.0 - sig))))).astype(BF16)
    return rows_in, cot_in, both_down, grads, act


def keeper_back(got, down, up, back):
    _, _, both_down, grads, _ = keeper_values(got, down, up)
    back[...] = lax.dot_general(grads, both_down, (((1,), (1,)), ((), ())), preferred_element_type=F32).astype(BF16)


def sum_last_rows(back, out):
    row = lax.broadcasted_iota(jnp.int32, (out.shape[0], back.shape[0]), 1)
    last = jnp.where(row % HALF == HALF - 1, 1.0, 0.0).astype(BF16)
    out[...] = jnp.dot(last, back[...], preferred_element_type=F32)


def keeper_grads(place, got, down_w, up_w, kept, given, act, down, up):
    parts, twice, _ = kept.shape
    part = twice // 2
    core = place[0] % 2
    rows_in, cot_in, _, grads, acts = keeper_values(got, down_w, up_w)
    act[...] = acts
    down[...] = lax.dot_general(rows_in, grads, (((0,), (0,)), ((), ())), preferred_element_type=F32)
    up[...] = lax.dot_general(cot_in, acts, (((0,), (0,)), ((), ())), preferred_element_type=F32)
    for at in range(parts):
        near = pl.ds(pl.multiple_of((2 * at + core) * part, part), part)
        far = pl.ds(pl.multiple_of((2 * at + 1 - core) * part, part), part)
        kept[at, :part] = down[near]
        kept[at, part:] = up[near]
        given[at, :part] = down[far].astype(BF16)
        given[at, part:] = up[far].astype(BF16)


def share_grads(place, kept, got, own, *given):
    chip = place[0] // 2
    for turn, out in enumerate((own,) + given):
        for high in range(out.shape[0]):
            at = 4 * high + ((chip % 4) ^ turn)
            out[high] = (kept[at] + got[at].astype(F32)).astype(out.dtype)


def pair_grads(place, own, first, second, third, kept, given):
    high = place[0] // 8
    for at, out in ((high, kept), (1 - high, given)):
        total = own[at] + first[at].astype(F32) + second[at].astype(F32) + third[at].astype(F32)
        out[...] = total.astype(out.dtype)


def sum_gradients(
    numbers, back, cot, summed, gain, left, own, right, act, up, total, low, high, sums, cells, frames_grad, inv
):
    frames, width = cot.shape
    gather = gather_matrix(segments(numbers), back.shape[0], frames)
    cells[:EDGE] = left[...].astype(F32)
    cells[EDGE : EDGE + frames] = own[...].astype(F32)
    cells[EDGE + frames :] = right[...].astype(F32)
    frames_grad[...] = jnp.dot(gather, back[...], preferred_element_type=F32)
    scale = lax.rsqrt(jnp.sum(summed[...] * summed[...], axis=1, keepdims=True) * (1.0 / width) + 1e-06)
    inv[...] = jnp.broadcast_to(scale, inv.shape)
    inner = jnp.sum(gain[...] * frames_grad[...] * summed[...], axis=1, keepdims=True) * (1.0 / width)
    pull = scale * scale * scale * inner
    half = frames // 2

    def column(at, carry):
        lanes = pl.ds(pl.multiple_of(at * LANES, LANES), LANES)
        for part in range(2):
            span = slice(part * half, part * half + half)
            grad = frames_grad[span, lanes]
            base = summed[span, lanes]
            inverse = inv[span, :]
            gain_sum = jnp.sum(grad * base * inverse, axis=0, keepdims=True)
            whole = cot[span, lanes].astype(F32) + inverse * (gain[:, lanes] * grad) - base * pull[span]
            total[span, lanes] = whole
            block = cells[part * half : part * half + half + 2 * EDGE, lanes]
            found = [None] * 31
            for low in range(8):
                moved = shifted(block, low)
                for high in range(0, 32, 8):
                    if high + low > 0:
                        product = whole * moved[high : high + half]
                        found[high + low - 1] = jnp.sum(product, axis=0, keepdims=True)
            rows = jnp.concatenate(found + [gain_sum], axis=0)
            if part == 0:
                first = rows
            else:
                sums[:, lanes] = first + rows
        return carry

    lax.fori_loop(0, width // LANES, column, 0)
    both_up = up[...].reshape(act.shape[1], width)
    count, blocks = act.shape[0], sums.shape[0]
    row = lax.broadcasted_iota(jnp.int32, (count, blocks), 0)
    block = lax.broadcasted_iota(jnp.int32, (count, blocks), 1)
    last = jnp.where(row == block * BLOCK + BLOCK - 1, 1.0, 0.0).astype(BF16)
    branch = jnp.dot(act[...], both_up, preferred_element_type=F32)
    branch = branch + jnp.dot(last, sums[...].astype(BF16), preferred_element_type=F32)
    branch = branch.reshape(blocks, BLOCK, width)
    low[...] = branch[:, :HALF].reshape(low.shape).astype(BF16)
    high[...] = branch[:, HALF:].reshape(high.shape).astype(BF16)


def input_gradient(left, own, right, taps, out, cells):
    frames, width = own.shape
    cells[:EDGE] = left[...]
    cells[EDGE : EDGE + frames] = own[...]
    cells[EDGE + frames :] = right[...]
    half = frames // 2

    def column(at, carry):
        lanes = pl.ds(pl.multiple_of(at * LANES, LANES), LANES)
        for part in range(2):
            block = cells[part * half : part * half + half + 2 * EDGE, lanes]
            total = block[EDGE : EDGE + half]
            for low in range(8):
                moved = shifted(block, low)
                for high in range(0, 32, 8):
                    if high + low > 0:
                        tap = taps[31 - high - low : 32 - high - low, lanes]
                        total = total + tap * moved[high : high + half]
            out[part * half : part * half + half, lanes] = total.astype(BF16)
        return carry

    lax.fori_loop(0, width // LANES, column, 0)


def add_branch(numbers, low, high, summed, out):
    frames = summed.shape[0]
    slot = frame_slots(segments(numbers), (frames, LANES), 0)
    lane = lax.broadcasted_iota(jnp.int32, (frames, LANES), 1)
    within = slot % BLOCK
    place = (slot // BLOCK) * HALF + within % HALF
    total = summed[...]
    for part, first in ((low, True), (high, False)):
        here = (within < HALF) if first else (within >= HALF)
        hits = [jnp.where(here & (lane + at == place), 1.0, 0.0) for at in range(0, part.shape[0], LANES)]
        total = total + jnp.dot(jnp.concatenate(hits, axis=1).astype(BF16), part[...], preferred_element_type=F32)
    out[...] = total.astype(BF16)


def place_grads(scale, kept, got, down, up):
    share, units = down.shape[1:]
    total = (kept[...] + got[...].astype(F32)) * scale
    for which in range(2):
        lanes = slice(which * units, which * units + units)
        down[which] = total[:share, lanes]
        up[which] = total[share:, lanes]


def from_sides(head, tail, axis):
    count = lax.axis_size(axis)
    left = lax.ppermute(tail, axis, [(i, i + 1) for i in range(count - 1)])
    right = lax.ppermute(head, axis, [(i + 1, i) for i in range(count - 1)])
    return left, right


def exchanged(blocks, axis, unit):
    count = lax.axis_size(axis)
    return [
        lax.ppermute(block, axis, [(i, i ^ (turn * unit)) for i in range(count)])
        for turn, block in enumerate(blocks[1:], 1)
    ]


def swap(cells, axis):
    return lax.all_to_all(cells, axis, split_axis=0, concat_axis=0, tiled=True)


def spread_rows(rows, axis):
    count = lax.axis_size(axis)
    return swap(jnp.broadcast_to(rows[None], (count,) + rows.shape), axis)


def local(
    inputs, cotangent, conv_kernel, norm_gain, adapt_down, adapt_up, segment_lengths, segment_langs, lang_slot
):
    frames, width = inputs.shape[1:]
    units = adapt_down.shape[2]
    dp, ctx = lax.axis_size("dp"), lax.axis_size("ctx")
    rows = ctx * BLOCK
    own, cot = inputs[0], cotangent[0]
    gain = norm_gain.reshape(1, width)
    numbers = jnp.concatenate([segment_lengths.reshape(-1), segment_langs.reshape(-1), lang_slot])
    where = [("s", numbers)]

    left, right = from_sides(own[:EDGE], own[frames - EDGE :], "ctx")
    send, summed = call(
        conv_and_norm,
        [((ctx, 2 * BLOCK, width), BF16), ((frames, width), F32)],
        where + [("v", left), ("v", own), ("v", right), ("v", cot), ("v", conv_kernel), ("v", gain)],
        [((frames + 2 * EDGE, width), F32), ((frames, width), BF16)],
    )
    got = swap(send, "ctx")
    (back,) = call(
        keeper_back, [((rows, width), BF16)], [("v", got), ("v", adapt_down), ("v", adapt_up)]
    )
    grad_back = swap(back, "ctx")
    share = width // dp
    place = ("s", lax.axis_index("dp").astype(jnp.int32).reshape(1))
    kept, given, act = call(
        keeper_grads,
        [((dp // 2, 2 * share, 2 * units), F32), ((dp // 2, 2 * share, 2 * units), BF16), ((rows, 2 * units), BF16)],
        [place, ("v", got), ("v", adapt_down), ("v", adapt_up)],
        [((width, 2 * units), F32), ((width, 2 * units), F32)],
    )
    (got,) = exchanged([kept, given], "dp", 1)
    grad_scale = 1.0 / math.sqrt(dp * ctx * frames)
    piece = (2 * share, 2 * units)
    chips = call(
        share_grads,
        [((2,) + piece, F32)] + [((2,) + piece, BF16)] * 3,
        [place, ("v", kept), ("v", got)],
    )
    got = exchanged(chips, "dp", 2)
    kept, given = call(
        pair_grads, [(piece, F32), (piece, BF16)], [place, ("v", chips[0])] + [("v", part) for part in got]
    )
    grad_back, kept, given = lax.optimization_barrier((grad_back, kept, given))
    total, low, high = call(
        sum_gradients,
        [((frames, width), F32), ((rows // 2, width), BF16), ((rows // 2, width), BF16)],
        where
        + [("v", grad_back), ("v", cot), ("v", summed), ("v", gain)]
        + [("v", left), ("v", own), ("v", right), ("v", act), ("v", adapt_up)],
        [((ctx, width), F32), ((frames + 2 * EDGE, width), F32), ((frames, width), F32), ((frames, LANES), F32)],
    )
    high_back = swap(high, "ctx")
    (got,) = exchanged([kept, given], "dp", 8)
    grad_down, grad_up = call(
        functools.partial(place_grads, grad_scale), [((2, share, units), F32)] * 2, [("v", kept), ("v", got)]
    )
    grad_left, grad_right = from_sides(total[:EDGE], total[frames - EDGE :], "ctx")
    high_back, low, grad_down, grad_up, grad_left, grad_right = lax.optimization_barrier(
        (high_back, low, grad_down, grad_up, grad_left, grad_right)
    )
    low_back = swap(low, "ctx")
    (mine,) = call(sum_last_rows, [((8, width), F32)], [("v", high_back)])
    mine = lax.all_gather(mine[:1], "dp", axis=0, tiled=True)
    (grad_input,) = call(
        input_gradient,
        [((frames, width), BF16)],
        [("v", grad_left), ("v", total), ("v", grad_right), ("v", conv_kernel)],
        [((frames + 2 * EDGE, width), F32)],
    )
    mine, low_back = lax.optimization_barrier((mine, low_back))
    mine = jnp.sum(mine, axis=0, keepdims=True) * grad_scale
    reduced = spread_rows(mine, "ctx").reshape(ctx, width)
    (output,) = call(
        add_branch,
        [((frames, width), BF16)],
        where + [("v", low_back), ("v", high_back), ("v", summed)],
    )
    return output[None], grad_input[None], reduced[:31], reduced[31], grad_down, jnp.transpose(grad_up, (0, 2, 1))


def solution(mesh):
    in_specs = (
        P("dp", "ctx", None),
        P("dp", "ctx", None),
        P(),
        P(),
        P("ctx", None, None),
        P("ctx", None, None),
        P("dp", "ctx", None),
        P("dp", "ctx", None),
        P(),
    )
    out_specs = (
        P("dp", "ctx", None),
        P("dp", "ctx", None),
        P(),
        P(),
        P("ctx", "dp", None),
        P("ctx", None, "dp"),
    )
    return jax.shard_map(local, mesh=mesh, in_specs=in_specs, out_specs=out_specs, check_vma=False)
```

```python
import functools
import math

import jax
import jax.numpy as jnp
from jax import lax
from jax.experimental import pallas as pl
from jax.experimental.pallas import tpu as pltpu
from jax.sharding import PartitionSpec as P

BLOCK = 16
HALF = BLOCK // 2
SEGMENTS = 16
EDGE = 16
LANES = 128
VMEM = pl.BlockSpec(memory_space=pltpu.VMEM)
SMEM = pl.BlockSpec(memory_space=pltpu.SMEM)
PARAMS = pltpu.CompilerParams(vmem_limit_bytes=40 * 1024 * 1024)
F32 = jnp.float32
BF16 = jnp.bfloat16


def call(body, outs, ins, scratch=()):
    return pl.pallas_call(
        body,
        out_shape=tuple(jax.ShapeDtypeStruct(shape, kind) for shape, kind in outs),
        in_specs=[SMEM if space == "s" else VMEM for space, _ in ins],
        out_specs=tuple(VMEM for _ in outs),
        scratch_shapes=[pltpu.VMEM(shape, kind) for shape, kind in scratch],
        compiler_params=PARAMS,
    )(*[array for _, array in ins])


def segments(numbers):
    start = jnp.int32(0)
    found = []
    for seg in range(SEGMENTS):
        slot = numbers[2 * SEGMENTS + numbers[SEGMENTS + seg]]
        end = start + numbers[seg]
        found.append((start, end, slot // 2, slot % 2))
        start = end
    return found


def frame_slots(found, shape, dim):
    frame = lax.broadcasted_iota(jnp.int32, shape, dim)
    slot = jnp.zeros(shape, jnp.int32)
    for start, end, keeper, _ in found:
        slot = jnp.where((frame >= start) & (frame < end), keeper * BLOCK - start + frame, slot)
    return slot


def scatter_matrix(found, rows, frames):
    slot = frame_slots(found, (1, frames), 1)
    row = lax.broadcasted_iota(jnp.int32, (rows, frames), 0)
    return jnp.where(row == slot, 1.0, 0.0).astype(BF16)


def gather_matrix(found, rows, frames):
    slot = frame_slots(found, (frames, LANES), 0)
    lane = lax.broadcasted_iota(jnp.int32, (frames, LANES), 1)
    parts = [jnp.where(lane + at == slot, 1.0, 0.0) for at in range(0, rows, LANES)]
    return jnp.concatenate(parts, axis=1).astype(BF16)


def shifted(cells, by):
    return cells if by == 0 else pltpu.roll(cells, cells.shape[0] - by, 0)


def conv_and_norm(numbers, left, own, right, cot, taps, gain, send, summed, cells, normed):
    frames, width = own.shape
    rows = send.shape[0] * BLOCK
    blocks = (send.shape[0], BLOCK, width)
    found = segments(numbers)
    spread = scatter_matrix(found, rows, frames)
    row = lax.broadcasted_iota(jnp.int32, (rows, LANES), 0)
    mark = jnp.zeros((rows, LANES), F32)
    for _, _, keeper, which in found:
        mark = jnp.where(row == keeper * BLOCK + BLOCK - 1, which.astype(F32), mark)
    moved = jnp.dot(spread, cot[...], preferred_element_type=F32)
    moved = jnp.concatenate([moved[:, :LANES] + mark, moved[:, LANES:]], axis=1)
    send[:, BLOCK:] = moved.astype(BF16).reshape(blocks)
    cells[:EDGE] = left[...].astype(F32)
    cells[EDGE : EDGE + frames] = own[...].astype(F32)
    cells[EDGE + frames :] = right[...].astype(F32)
    half = frames // 2

    def column(at, squares):
        lanes = pl.ds(pl.multiple_of(at * LANES, LANES), LANES)
        sums = []
        for part in range(2):
            block = cells[part * half : part * half + half + 2 * EDGE, lanes]
            total = block[EDGE : EDGE + half]
            for low in range(8):
                moved = shifted(block, low)
                for high in range(0, 32, 8):
                    if high + low > 0:
                        tap = taps[high + low - 1 : high + low, lanes]
                        total = total + tap * moved[high : high + half]
            summed[part * half : part * half + half, lanes] = total
            sums.append(total * total)
        return squares + jnp.concatenate(sums, axis=0)

    squares = lax.fori_loop(0, width // LANES, column, jnp.zeros((frames, LANES), F32))
    scale = lax.rsqrt(jnp.sum(squares, axis=1, keepdims=True) * (1.0 / width) + 1e-06)
    normed[...] = (summed[...] * scale * gain[...]).astype(BF16)
    send[:, :BLOCK] = jnp.dot(spread, normed[...], preferred_element_type=F32).astype(BF16).reshape(blocks)


def received(got):
    shape = (got.shape[0] * BLOCK, got.shape[2])
    return got[:, :BLOCK].reshape(shape), got[:, BLOCK:].reshape(shape)


def keeper_values(got, down, up):
    rows_in, cot_in = received(got)
    rows, width = rows_in.shape
    units = down.shape[2]
    marks = cot_in[:, :units].astype(F32).reshape(rows // BLOCK, BLOCK, units)
    marks = jnp.broadcast_to(marks[:, BLOCK - 1 :, :], marks.shape).reshape(rows, units)
    keep = jnp.concatenate([1.0 - marks, marks], axis=1)
    both_down = jnp.concatenate([down[0], down[1]], axis=1)
    both_up = up[...].reshape(2 * units, width)
    pre = jnp.dot(rows_in, both_down, preferred_element_type=F32)
    slope_of = lax.dot_general(cot_in, both_up, (((1,), (1,)), ((), ())), preferred_element_type=F32)
    sig = jax.nn.sigmoid(pre)
    act = (keep * (pre * sig)).astype(BF16)
    grads = (keep * (slope_of * (sig * (1.0 + pre * (1.0 - sig))))).astype(BF16)
    return rows_in, cot_in, both_down, grads, act


def keeper_back(got, down, up, back):
    _, _, both_down, grads, _ = keeper_values(got, down, up)
    back[...] = lax.dot_general(grads, both_down, (((1,), (1,)), ((), ())), preferred_element_type=F32).astype(BF16)


def keeper_low(act, up, low):
    count, width = act.shape[0], low.shape[1]
    branch = jnp.dot(act[...], up[...].reshape(act.shape[1], width), preferred_element_type=F32)
    low[...] = branch.reshape(count // BLOCK, BLOCK, width)[:, :HALF].reshape(low.shape).astype(BF16)


def sum_last_rows(back, out):
    row = lax.broadcasted_iota(jnp.int32, (out.shape[0], back.shape[0]), 1)
    last = jnp.where(row % HALF == HALF - 1, 1.0, 0.0).astype(BF16)
    out[...] = jnp.dot(last, back[...], preferred_element_type=F32)


def keeper_grads(place, got, down_w, up_w, kept, given, act, down, up):
    parts, twice, _ = kept.shape
    part = twice // 2
    core = place[0] % 2
    rows_in, cot_in, _, grads, acts = keeper_values(got, down_w, up_w)
    act[...] = acts
    down[...] = lax.dot_general(rows_in, grads, (((0,), (0,)), ((), ())), preferred_element_type=F32)
    up[...] = lax.dot_general(cot_in, acts, (((0,), (0,)), ((), ())), preferred_element_type=F32)
    for at in range(parts):
        near = pl.ds(pl.multiple_of((2 * at + core) * part, part), part)
        far = pl.ds(pl.multiple_of((2 * at + 1 - core) * part, part), part)
        kept[at, :part] = down[near]
        kept[at, part:] = up[near]
        given[at, :part] = down[far].astype(BF16)
        given[at, part:] = up[far].astype(BF16)


def share_grads(place, kept, got, own, *given):
    chip = place[0] // 2
    for turn, out in enumerate((own,) + given):
        for high in range(out.shape[0]):
            at = 4 * high + ((chip % 4) ^ turn)
            out[high] = (kept[at] + got[at].astype(F32)).astype(out.dtype)


def pair_grads(place, own, first, second, third, kept, given):
    high = place[0] // 8
    for at, out in ((high, kept), (1 - high, given)):
        total = own[at] + first[at].astype(F32) + second[at].astype(F32) + third[at].astype(F32)
        out[...] = total.astype(out.dtype)


def sum_gradients(
    numbers, back, cot, summed, gain, left, own, right, act, up, total, high, sums, cells, frames_grad, inv
):
    frames, width = cot.shape
    gather = gather_matrix(segments(numbers), back.shape[0], frames)
    cells[:EDGE] = left[...].astype(F32)
    cells[EDGE : EDGE + frames] = own[...].astype(F32)
    cells[EDGE + frames :] = right[...].astype(F32)
    frames_grad[...] = jnp.dot(gather, back[...], preferred_element_type=F32)
    scale = lax.rsqrt(jnp.sum(summed[...] * summed[...], axis=1, keepdims=True) * (1.0 / width) + 1e-06)
    inv[...] = jnp.broadcast_to(scale, inv.shape)
    inner = jnp.sum(gain[...] * frames_grad[...] * summed[...], axis=1, keepdims=True) * (1.0 / width)
    pull = scale * scale * scale * inner
    half = frames // 2

    def column(at, carry):
        lanes = pl.ds(pl.multiple_of(at * LANES, LANES), LANES)
        for part in range(2):
            span = slice(part * half, part * half + half)
            grad = frames_grad[span, lanes]
            base = summed[span, lanes]
            inverse = inv[span, :]
            gain_sum = jnp.sum(grad * base * inverse, axis=0, keepdims=True)
            whole = cot[span, lanes].astype(F32) + inverse * (gain[:, lanes] * grad) - base * pull[span]
            total[span, lanes] = whole
            block = cells[part * half : part * half + half + 2 * EDGE, lanes]
            found = [None] * 31
            for low in range(8):
                moved = shifted(block, low)
                for high in range(0, 32, 8):
                    if high + low > 0:
                        product = whole * moved[high : high + half]
                        found[high + low - 1] = jnp.sum(product, axis=0, keepdims=True)
            rows = jnp.concatenate(found + [gain_sum], axis=0)
            if part == 0:
                first = rows
            else:
                sums[:, lanes] = first + rows
        return carry

    lax.fori_loop(0, width // LANES, column, 0)
    both_up = up[...].reshape(act.shape[1], width)
    count, blocks = act.shape[0], sums.shape[0]
    row = lax.broadcasted_iota(jnp.int32, (count, blocks), 0)
    block = lax.broadcasted_iota(jnp.int32, (count, blocks), 1)
    last = jnp.where(row == block * BLOCK + BLOCK - 1, 1.0, 0.0).astype(BF16)
    branch = jnp.dot(act[...], both_up, preferred_element_type=F32)
    branch = branch + jnp.dot(last, sums[...].astype(BF16), preferred_element_type=F32)
    branch = branch.reshape(blocks, BLOCK, width)
    high[...] = branch[:, HALF:].reshape(high.shape).astype(BF16)


def input_gradient(left, own, right, taps, out, cells):
    frames, width = own.shape
    cells[:EDGE] = left[...]
    cells[EDGE : EDGE + frames] = own[...]
    cells[EDGE + frames :] = right[...]
    half = frames // 2

    def column(at, carry):
        lanes = pl.ds(pl.multiple_of(at * LANES, LANES), LANES)
        for part in range(2):
            block = cells[part * half : part * half + half + 2 * EDGE, lanes]
            total = block[EDGE : EDGE + half]
            for low in range(8):
                moved = shifted(block, low)
                for high in range(0, 32, 8):
                    if high + low > 0:
                        tap = taps[31 - high - low : 32 - high - low, lanes]
                        total = total + tap * moved[high : high + half]
            out[part * half : part * half + half, lanes] = total.astype(BF16)
        return carry

    lax.fori_loop(0, width // LANES, column, 0)


def add_branch(numbers, low, high, summed, out):
    frames = summed.shape[0]
    slot = frame_slots(segments(numbers), (frames, LANES), 0)
    lane = lax.broadcasted_iota(jnp.int32, (frames, LANES), 1)
    within = slot % BLOCK
    place = (slot // BLOCK) * HALF + within % HALF
    total = summed[...]
    for part, first in ((low, True), (high, False)):
        here = (within < HALF) if first else (within >= HALF)
        hits = [jnp.where(here & (lane + at == place), 1.0, 0.0) for at in range(0, part.shape[0], LANES)]
        total = total + jnp.dot(jnp.concatenate(hits, axis=1).astype(BF16), part[...], preferred_element_type=F32)
    out[...] = total.astype(BF16)


def place_grads(scale, kept, got, down, up):
    share, units = down.shape[1:]
    total = (kept[...] + got[...].astype(F32)) * scale
    for which in range(2):
        lanes = slice(which * units, which * units + units)
        down[which] = total[:share, lanes]
        up[which] = total[share:, lanes]


def from_sides(head, tail, axis):
    count = lax.axis_size(axis)
    left = lax.ppermute(tail, axis, [(i, i + 1) for i in range(count - 1)])
    right = lax.ppermute(head, axis, [(i + 1, i) for i in range(count - 1)])
    return left, right


def exchanged(blocks, axis, unit):
    count = lax.axis_size(axis)
    return [
        lax.ppermute(block, axis, [(i, i ^ (turn * unit)) for i in range(count)])
        for turn, block in enumerate(blocks[1:], 1)
    ]


def swap(cells, axis):
    return lax.all_to_all(cells, axis, split_axis=0, concat_axis=0, tiled=True)


def spread_rows(rows, axis):
    count = lax.axis_size(axis)
    return swap(jnp.broadcast_to(rows[None], (count,) + rows.shape), axis)


def local(
    inputs, cotangent, conv_kernel, norm_gain, adapt_down, adapt_up, segment_lengths, segment_langs, lang_slot
):
    frames, width = inputs.shape[1:]
    units = adapt_down.shape[2]
    dp, ctx = lax.axis_size("dp"), lax.axis_size("ctx")
    rows = ctx * BLOCK
    own, cot = inputs[0], cotangent[0]
    gain = norm_gain.reshape(1, width)
    numbers = jnp.concatenate([segment_lengths.reshape(-1), segment_langs.reshape(-1), lang_slot])
    where = [("s", numbers)]

    left, right = from_sides(own[:EDGE], own[frames - EDGE :], "ctx")
    send, summed = call(
        conv_and_norm,
        [((ctx, 2 * BLOCK, width), BF16), ((frames, width), F32)],
        where + [("v", left), ("v", own), ("v", right), ("v", cot), ("v", conv_kernel), ("v", gain)],
        [((frames + 2 * EDGE, width), F32), ((frames, width), BF16)],
    )
    got = swap(send, "ctx")
    (back,) = call(
        keeper_back, [((rows, width), BF16)], [("v", got), ("v", adapt_down), ("v", adapt_up)]
    )
    grad_back = swap(back, "ctx")
    share = width // dp
    place = ("s", lax.axis_index("dp").astype(jnp.int32).reshape(1))
    kept, given, act = call(
        keeper_grads,
        [((dp // 2, 2 * share, 2 * units), F32), ((dp // 2, 2 * share, 2 * units), BF16), ((rows, 2 * units), BF16)],
        [place, ("v", got), ("v", adapt_down), ("v", adapt_up)],
        [((width, 2 * units), F32), ((width, 2 * units), F32)],
    )
    (got,) = exchanged([kept, given], "dp", 1)
    grad_scale = 1.0 / math.sqrt(dp * ctx * frames)
    piece = (2 * share, 2 * units)
    chips = call(
        share_grads,
        [((2,) + piece, F32)] + [((2,) + piece, BF16)] * 3,
        [place, ("v", kept), ("v", got)],
    )
    got = exchanged(chips, "dp", 2)
    kept, given = call(
        pair_grads, [(piece, F32), (piece, BF16)], [place, ("v", chips[0])] + [("v", part) for part in got]
    )
    grad_back, kept, given = lax.optimization_barrier((grad_back, kept, given))
    total, high = call(
        sum_gradients,
        [((frames, width), F32), ((rows // 2, width), BF16)],
        where
        + [("v", grad_back), ("v", cot), ("v", summed), ("v", gain)]
        + [("v", left), ("v", own), ("v", right), ("v", act), ("v", adapt_up)],
        [((ctx, width), F32), ((frames + 2 * EDGE, width), F32), ((frames, width), F32), ((frames, LANES), F32)],
    )
    (low,) = call(keeper_low, [((rows // 2, width), BF16)], [("v", act), ("v", adapt_up)])
    high_back = swap(high, "ctx")
    (got,) = exchanged([kept, given], "dp", 8)
    grad_down, grad_up = call(
        functools.partial(place_grads, grad_scale), [((2, share, units), F32)] * 2, [("v", kept), ("v", got)]
    )
    grad_left, grad_right = from_sides(total[:EDGE], total[frames - EDGE :], "ctx")
    high_back, low, grad_down, grad_up, grad_left, grad_right = lax.optimization_barrier(
        (high_back, low, grad_down, grad_up, grad_left, grad_right)
    )
    low_back = swap(low, "ctx")
    (mine,) = call(sum_last_rows, [((8, width), F32)], [("v", high_back)])
    mine = lax.all_gather(mine[:1], "dp", axis=0, tiled=True)
    (grad_input,) = call(
        input_gradient,
        [((frames, width), BF16)],
        [("v", grad_left), ("v", total), ("v", grad_right), ("v", conv_kernel)],
        [((frames + 2 * EDGE, width), F32)],
    )
    mine, low_back = lax.optimization_barrier((mine, low_back))
    mine = jnp.sum(mine, axis=0, keepdims=True) * grad_scale
    reduced = spread_rows(mine, "ctx").reshape(ctx, width)
    (output,) = call(
        add_branch,
        [((frames, width), BF16)],
        where + [("v", low_back), ("v", high_back), ("v", summed)],
    )
    return output[None], grad_input[None], reduced[:31], reduced[31], grad_down, jnp.transpose(grad_up, (0, 2, 1))


def solution(mesh):
    in_specs = (
        P("dp", "ctx", None),
        P("dp", "ctx", None),
        P(),
        P(),
        P("ctx", None, None),
        P("ctx", None, None),
        P("dp", "ctx", None),
        P("dp", "ctx", None),
        P(),
    )
    out_specs = (
        P("dp", "ctx", None),
        P("dp", "ctx", None),
        P(),
        P(),
        P("ctx", "dp", None),
        P("ctx", None, "dp"),
    )
    return jax.shard_map(local, mesh=mesh, in_specs=in_specs, out_specs=out_specs, check_vma=False)
```
